512 devices in a mesh: dp: 16 (over y, x_hi), ctx: 8 (over z), tp: 4 (over x_lo, core).
Axes of the slice: x: 4 (x_hi: 2, x_lo: 2; x = x_hi * 2 + x_lo), y: 8, z: 8, core: 2. Of those that a mesh axis runs over, the one named last changes fastest.
Arguments:
- queries: bfloat16 [32768, 1280], P(('dp', 'ctx'), 'tp'), may hold values from -300 to 300, as said below
- keys: bfloat16 [32768, 1280], P(('dp', 'ctx'), 'tp'), may hold values from -7 to 7, as said below
- values: bfloat16 [32768, 1280], P(('dp', 'ctx'), 'tp'), may hold values from -6 to 6
- saved_out: bfloat16 [32768, 1280], P(('dp', 'ctx'), 'tp'), may hold values from -6 to 6
- cotangent: bfloat16 [32768, 1280], P(('dp', 'ctx'), 'tp'), may hold values from -24 to 24
- proj_weight: bfloat16 [1280, 1280], P('tp'), may hold values from -0.15625 to 0.15625
Outputs:
- query_grad: bfloat16 [32768, 1280], P(('dp', 'ctx'), 'tp')
- key_grad: bfloat16 [32768, 1280], P(('dp', 'ctx'), 'tp')
- value_grad: bfloat16 [32768, 1280], P(('dp', 'ctx'), 'tp')
- proj_grad: float32 [1280, 1280], P('tp', ('dp', 'ctx'))
The draws below stay inside these ranges and needn't reach their ends.
Inputs may be any that keep to these rules, and one draw needn't show every extreme that they name: `keys`: keys of order one. `queries`: Queries; some rows may be far larger than others.
All inputs are finite; a program needn't handle non-finite values.
Results may differ from the reference program's by a relative error of at most 0.014.
Values may be sent and summed in bfloat16 or wider, within the bound.
No kernel may reach another device: no remote copies, remote signals or barrier semaphores. Data moves between devices by JAX's collectives and lax.ppermute only.
A program may use at most 64 MiB of HBM per device.

```python
import jax
import jax.numpy as jnp
from jax import lax

D = 1280
HEADS = 16
HD = 80
TOKENS = 2048
IMAGES = 16
ROWS = 32768


def base_keys(key):
    return jnp.clip(jax.random.normal(key, (ROWS, D), jnp.float32), -6.0, 6.0)


def draw_keys(key, part):
    base = base_keys(key)
    return base.astype(jnp.bfloat16)


def draw_queries(key, part):
    key = jax.random.fold_in(key, 23)
    fresh = jnp.clip(jax.random.normal(key, (ROWS, D), jnp.float32), -6.0, 6.0)
    return fresh.astype(jnp.bfloat16)


def spiked(entries, rng, source, target, parts, factor):
    owner, partner = [(jnp.arange(entries.shape[dim]) // (entries.shape[dim] // parts)).reshape([-1 if axis == dim else 1 for axis in range(entries.ndim)]) for dim in (source, target)]
    chosen = jax.random.permutation(rng, parts)[partner]
    strong = (owner == chosen) | (owner == (partner + parts // 2) % parts)
    return jnp.where(strong, factor * entries, entries)


def block_scale(stream_key, shape, shards, least, largest):
    def one(position, shards_of):
        draws = jax.random.uniform(jax.random.fold_in(jax.random.fold_in(stream_key, 6), position), (shards_of,), jnp.float32, least / len(shards), largest / len(shards))
        return jnp.repeat(jnp.exp(draws), shape[position] // shards_of).reshape((-1,) + (1,) * (len(shape) - position - 1))

    level = one(*shards[0])
    for cut in shards[1:]:
        level = level * one(*cut)
    return level


def normal_values(own_key, extent, width, reach, shards=(), kind=jnp.bfloat16):
    drawn = jax.random.normal(own_key, extent, jnp.float32) * width
    if len(shards) > 0:
        drawn = block_scale(own_key, extent, shards, -0.22, 0.18) * drawn
    return jnp.clip(drawn, min=-reach, max=reach).astype(kind)


def heavy_noise(rng, dims, scale, reach, pieces, heavy, dtype=jnp.bfloat16):
    entries = scale * jax.random.normal(rng, dims, jnp.float32)
    if pieces:
        entries = entries * block_scale(rng, dims, pieces, -0.22, 0.18)
    return jnp.clip(spiked(entries, jax.random.fold_in(rng, 3), *heavy), -reach, reach).astype(dtype)


def setup_inputs(seed: int = 0) -> dict:
    key_list = jax.random.split(jax.random.key(seed), 7)
    queries = draw_queries(jax.random.fold_in(key_list[6], 71), 0)
    keys = draw_keys(jax.random.fold_in(key_list[6], 71), 0)
    values = normal_values(key_list[2], (ROWS, D), 1.0, 6.0, ((0, 128), (1, 4)))
    saved_out = normal_values(key_list[3], (ROWS, D), 1.0, 6.0, ((0, 128), (1, 4)))
    cotangent = heavy_noise(key_list[4], (ROWS, D), 1.0, 24.0, ((0, 128), (1, 4)), (0, 1, 128, 5.5))
    proj_weight = normal_values(key_list[5], (D, D), D ** -0.5, 0.15625, ((0, 4),))
    return {"queries": queries, "keys": keys, "values": values, "saved_out": saved_out, "cotangent": cotangent, "proj_weight": proj_weight}


def dot32(left, right):
    return jnp.dot(left.astype(jnp.float32), right.astype(jnp.float32), preferred_element_type=jnp.float32)


def head_grads(pack):
    query, key_rows, value_rows, attn_grad, saved = pack
    factor = HD ** -0.5
    scores = dot32(query, key_rows.T) * factor
    peak = jnp.max(scores, axis=1, keepdims=True)
    lse = peak + jnp.log(jnp.sum(jnp.exp(scores - peak), axis=1, keepdims=True))
    prob = jnp.exp(scores - lse)
    delta = jnp.sum(attn_grad.astype(jnp.float32) * saved.astype(jnp.float32), axis=1, keepdims=True)
    dprob = dot32(attn_grad, value_rows.T)
    dscore = (factor * prob * (dprob - delta)).astype(jnp.bfloat16)
    query_part = dot32(dscore, key_rows).astype(jnp.bfloat16)
    key_part = dot32(dscore.T, query).astype(jnp.bfloat16)
    value_part = dot32(prob.astype(jnp.bfloat16).T, attn_grad).astype(jnp.bfloat16)
    return query_part, key_part, value_part


def to_heads(rows):
    return rows.reshape(IMAGES, TOKENS, HEADS, HD).transpose(0, 2, 1, 3).reshape(IMAGES * HEADS, TOKENS, HD)


def to_rows(heads):
    return heads.reshape(IMAGES, HEADS, TOKENS, HD).transpose(0, 2, 1, 3).reshape(IMAGES * TOKENS, HEADS * HD)


def reference(queries, keys, values, saved_out, cotangent, proj_weight):
    d_attn = dot32(cotangent, proj_weight.T).astype(jnp.bfloat16)
    proj_grad = dot32(saved_out.T, cotangent)
    grads = lax.map(head_grads, (to_heads(queries), to_heads(keys), to_heads(values), to_heads(d_attn), to_heads(saved_out)))
    return to_rows(grads[0]), to_rows(grads[1]), to_rows(grads[2]), proj_grad
```

```python
import functools
import math

import jax
import jax.numpy as jnp
from jax import lax
from jax.experimental import pallas as pl
from jax.experimental.pallas import tpu as pltpu
from jax.sharding import PartitionSpec as P

HD = 80
HEADS_HERE = 4
SHARDS = 8
ROWS = 256
HALF = 128
WIDE = HEADS_HERE * HD
FACTOR = HD ** (-0.5)
LOG2E = math.log2(math.e)
Q_AT, G_AT, K_AT, V_AT, IN_ROWS = 0, 80, 176, 336, 496
EXT = 96
DK_AT, DV_AT, PG_AT, OUT_ROWS = 80, 240, 400, 448
PG_COLS = 10

NT = (((1,), (1,)), ((), ()))
TN = (((0,), (0,)), ((), ()))
NN = (((1,), (0,)), ((), ()))


def dot(left, right, dims):
    return lax.dot_general(left, right, dims, preferred_element_type=jnp.float32)


def turned(block):
    return block.astype(jnp.float32).T.astype(jnp.bfloat16)


def pack_kernel(q_ref, k_ref, v_ref, o_ref, cot_ref, w_ref, out_ref):
    grad = dot(w_ref[...], cot_ref[...], NT).astype(jnp.bfloat16)
    out_t = o_ref[...].astype(jnp.float32).T
    q_t, k_t, v_t = turned(q_ref[...]), turned(k_ref[...]), turned(v_ref[...])
    for j in range(HEADS_HERE):
        cols = slice(j * HD, (j + 1) * HD)
        g = grad[cols]
        delta = jnp.sum(g.astype(jnp.float32) * out_t[cols], axis=0, keepdims=True)
        high = delta.astype(jnp.bfloat16).astype(jnp.float32)
        rest = delta - high
        middle = rest.astype(jnp.bfloat16).astype(jnp.float32)
        low = rest - middle
        row = lax.broadcasted_iota(jnp.int32, (EXT - HD, ROWS), 0)
        extra = jnp.where(
            row == 0, high, jnp.where(row == 1, middle, jnp.where(row == 2, low, 0.0))
        ).astype(jnp.bfloat16)
        for h in range(2):
            slot = out_ref.at[h * HEADS_HERE + j]
            mine = slice(h * HALF, (h + 1) * HALF)
            slot[Q_AT : Q_AT + HD] = q_t[cols, mine]
            slot[G_AT : G_AT + HD] = g[:, mine]
            slot[G_AT + HD : G_AT + EXT] = extra[:, mine]
            for b in range(2):
                tokens = slice(b * HALF, (b + 1) * HALF)
                slot[K_AT + b * HD : K_AT + (b + 1) * HD] = k_t[cols, tokens]
                slot[V_AT + b * HD : V_AT + (b + 1) * HD] = v_t[cols, tokens]


def grad_kernel(x_ref, pg_ref, out_ref, k_t, v_t, dk, dv):
    for s in range(SHARDS):
        for b in range(2):
            tokens = slice((2 * s + b) * HALF, (2 * s + b + 1) * HALF)
            k_t[:, tokens] = x_ref[s, K_AT + b * HD : K_AT + (b + 1) * HD]
            v_t[:HD, tokens] = x_ref[s, V_AT + b * HD : V_AT + (b + 1) * HD]
    row = lax.broadcasted_iota(jnp.int32, (EXT - HD, SHARDS * ROWS), 0)
    v_t[HD:] = jnp.where(row < 3, -1.0, 0.0).astype(jnp.bfloat16)
    for i in range(SHARDS // 2):
        q = jnp.concatenate([x_ref[2 * i + e, Q_AT : Q_AT + HD] for e in range(2)], axis=1)
        g = jnp.concatenate([x_ref[2 * i + e, G_AT : G_AT + EXT] for e in range(2)], axis=1)
        scores = dot(q, k_t[...], TN)
        peak = jnp.max(scores, axis=1, keepdims=True) * (FACTOR * LOG2E)
        raised = jnp.exp2(scores * (FACTOR * LOG2E) - peak)
        prob = raised * (1.0 / jnp.sum(raised, axis=1, keepdims=True))
        shifted = dot(g, v_t[...], TN)
        dscore = (prob * shifted).astype(jnp.bfloat16)
        dv_part = dot(g[:HD], prob.astype(jnp.bfloat16), NN)
        dk_part = dot(q, dscore, NN)
        if i == 0:
            dv[...] = dv_part
            dk[...] = dk_part
        else:
            dv[...] += dv_part
            dk[...] += dk_part
        dq = (dot(k_t[...], dscore, NT) * FACTOR).astype(jnp.bfloat16)
        for e in range(2):
            out_ref[2 * i + e, :HD] = dq[:, e * HALF : (e + 1) * HALF]
    for s in range(SHARDS):
        for b in range(2):
            tokens = slice((2 * s + b) * HALF, (2 * s + b + 1) * HALF)
            at = b * HD
            out_ref[s, DK_AT + at : DK_AT + at + HD] = (dk[:, tokens] * FACTOR).astype(jnp.bfloat16)
            out_ref[s, DV_AT + at : DV_AT + at + HD] = dv[:, tokens].astype(jnp.bfloat16)
        out_ref[s, PG_AT:] = pg_ref[s]


def unpack_kernel(x_ref, dq_ref, dk_ref, dv_ref, pg_ref):
    def both(j, at):
        return x_ref[j, at : at + HD].astype(jnp.float32), x_ref[
            HEADS_HERE + j, at : at + HD
        ].astype(jnp.float32)

    def put(ref, heads):
        ref[...] = jnp.concatenate(heads, axis=0).T.astype(jnp.bfloat16)

    put(dq_ref, [jnp.concatenate(both(j, 0), axis=1) for j in range(HEADS_HERE)])
    for ref, start in ((dk_ref, DK_AT), (dv_ref, DV_AT)):
        heads = []
        for j in range(HEADS_HERE):
            low = both(j, start)
            high = both(j, start + HD)
            heads.append(jnp.concatenate([low[0] + low[1], high[0] + high[1]], axis=1))
        put(ref, heads)
    total = x_ref[0, PG_AT:].astype(jnp.float32)
    for s in range(1, SHARDS):
        total = total + x_ref[s, PG_AT:].astype(jnp.float32)
    wide = jnp.concatenate([total[16 * c : 16 * (c + 1)] for c in range(3)], axis=1)
    pg_ref[...] = wide.T[:WIDE, :PG_COLS]


def call(kernel, outs, flops, transcendentals=0, scratch=()):
    return pl.pallas_call(
        kernel,
        out_shape=outs,
        scratch_shapes=scratch,
        compiler_params=pltpu.CompilerParams(vmem_limit_bytes=48 * 1024 * 1024),
        cost_estimate=pl.CostEstimate(
            flops=flops, bytes_accessed=2 * 1024 * 1024, transcendentals=transcendentals
        ),
    )


def on_device(queries, keys, values, saved_out, cotangent, proj_weight):
    half = jnp.bfloat16
    full_cot = lax.all_gather(cotangent, "tp", axis=1, tiled=True)
    packed = call(
        pack_kernel,
        jax.ShapeDtypeStruct((SHARDS, IN_ROWS, HALF), half),
        2 * ROWS * WIDE * 4 * WIDE,
    )(queries, keys, values, saved_out, full_cot, proj_weight)
    arrived = lax.all_to_all(packed, "ctx", 0, 0, tiled=True)

    term = dot(full_cot, saved_out, TN).astype(half)
    along_y = [[2 * y + x for y in range(8)] for x in range(2)]
    share = lax.psum_scatter(
        term, "dp", scatter_dimension=0, tiled=True, axis_index_groups=along_y
    )
    upper = lax.axis_index("dp") % 2
    lower_part, upper_part = share[:80], share[80:]
    kept = jnp.where(upper == 1, upper_part, lower_part).astype(jnp.float32)
    given = jnp.where(upper == 1, lower_part, upper_part)
    taken = lax.ppermute(given, "dp", [(i, i ^ 1) for i in range(16)])
    share = (kept + taken.astype(jnp.float32)).astype(half)
    share = jnp.pad(share.reshape(SHARDS, PG_COLS, WIDE), ((0, 0), (0, 6), (0, 64)))
    share = share.reshape(SHARDS, 16, 3, HALF).transpose(0, 2, 1, 3)
    share = share.reshape(SHARDS, OUT_ROWS - PG_AT, HALF)

    tokens = SHARDS * ROWS
    sent = call(
        grad_kernel,
        jax.ShapeDtypeStruct((SHARDS, OUT_ROWS, HALF), half),
        5 * 2 * tokens * (tokens // 2) * HD,
        tokens * (tokens // 2),
        [
            pltpu.VMEM((HD, tokens), half),
            pltpu.VMEM((EXT, tokens), half),
            pltpu.VMEM((HD, tokens), jnp.float32),
            pltpu.VMEM((HD, tokens), jnp.float32),
        ],
    )(arrived, share)
    back = lax.all_to_all(sent, "ctx", 0, 0, tiled=True)
    grad = jax.ShapeDtypeStruct((ROWS, WIDE), half)
    return call(
        unpack_kernel,
        (grad, grad, grad, jax.ShapeDtypeStruct((WIDE, PG_COLS), jnp.float32)),
        0,
    )(back)


def solution(mesh):
    rows = P(("dp", "ctx"), "tp")
    return jax.shard_map(
        on_device,
        mesh=mesh,
        in_specs=(rows, rows, rows, rows, rows, P("tp", None)),
        out_specs=(rows, rows, rows, P("tp", ("dp", "ctx"))),
        check_vma=False,
    )
```

```python
import math

import jax
import jax.numpy as jnp
from jax import lax
from jax.experimental import pallas as pl
from jax.experimental.pallas import tpu as pltpu
from jax.sharding import PartitionSpec as P

HD = 80
HEADS_HERE = 4
SHARDS = 8
DP = 16
ROWS = 256
HALF = 128
WIDE = HEADS_HERE * HD
FACTOR = HD ** (-0.5)
LOG2E = math.log2(math.e)
EXT = 96
QG_ROWS = HD + EXT
K_AT, V_AT, KV_ROWS = 0, 2 * HD, 4 * HD
PG_AT, OUT_ROWS = 4 * HD, 4 * HD + 48
PG_COLS = 10
PG_ROWS = 80
PG_USED = 208
NEAR = (0, 6, 1, 7)

NT = (((1,), (1,)), ((), ()))
TN = (((0,), (0,)), ((), ()))
NN = (((1,), (0,)), ((), ()))


def dot(left, right, dims):
    return lax.dot_general(left, right, dims, preferred_element_type=jnp.float32)


def pack_keys_kernel(k_hbm, v_hbm, out_ref, k_ref, v_ref, sems):
    pairs = ((k_hbm, k_ref), (v_hbm, v_ref))
    copies = [pltpu.make_async_copy(x, y, sems.at[i]) for i, (x, y) in enumerate(pairs)]
    for copy in copies:
        copy.start()
    for copy, ref, first in zip(copies, (k_ref, v_ref), (K_AT, V_AT)):
        copy.wait()
        for s in range(SHARDS):
            j = s % HEADS_HERE
            for b in range(2):
                at = first + b * HD
                out_ref[s, at : at + HD] = ref[j * HD : (j + 1) * HD, b * HALF : (b + 1) * HALF]


def pack_queries_and_proj_kernel(q_hbm, o_hbm, cot_ref, w_ref, *refs):
    out_refs, (out_ref, q_ref, o_ref, g_ref, extra_ref, sems) = refs[: len(NEAR)], refs[len(NEAR) :]
    pairs = ((q_hbm, q_ref), (o_hbm, o_ref))
    copies = [pltpu.make_async_copy(x, y, sems.at[i]) for i, (x, y) in enumerate(pairs)]
    for copy in copies:
        copy.start()
    g_ref[...] = dot(w_ref[...], cot_ref[...], NN).astype(jnp.bfloat16)
    for copy in copies:
        copy.wait()
    for j in range(HEADS_HERE):
        cols = slice(j * HD, (j + 1) * HD)
        delta = jnp.sum(
            g_ref[cols].astype(jnp.float32) * o_ref[cols].astype(jnp.float32),
            axis=0,
            keepdims=True,
        )
        high = delta.astype(jnp.bfloat16).astype(jnp.float32)
        rest = delta - high
        middle = rest.astype(jnp.bfloat16).astype(jnp.float32)
        low = rest - middle
        row = lax.broadcasted_iota(jnp.int32, (EXT - HD, ROWS), 0)
        extra = jnp.where(
            row == 0, high, jnp.where(row == 1, middle, jnp.where(row == 2, low, 0.0))
        )
        extra_ref[j * (EXT - HD) : (j + 1) * (EXT - HD)] = extra.astype(jnp.bfloat16)
    here = lax.axis_index("ctx")
    for away, ref in zip(NEAR, out_refs):
        j = lax.rem(here + away, HEADS_HERE)
        cols = pl.ds(pl.multiple_of(j * HD, 16), HD)
        ref[:HD] = q_ref[cols]
        ref[HD : 2 * HD] = g_ref[cols]
        rows = pl.ds(pl.multiple_of(j * (EXT - HD), 16), EXT - HD)
        ref[2 * HD :] = extra_ref[rows]
    empty = jnp.zeros((PG_USED - 200, HALF), jnp.float32)
    for d in range(DP):
        part = dot(cot_ref[d * PG_ROWS : (d + 1) * PG_ROWS], o_ref[...], NT)
        for c in range(2):
            at = c * PG_ROWS
            out_ref[d, at : at + PG_ROWS] = part[:, HALF * c : HALF * (c + 1)].astype(out_ref.dtype)
        last = part[:, 2 * HALF :]
        last = jnp.concatenate([last[: PG_ROWS // 2], last[PG_ROWS // 2 :]], axis=1)
        out_ref[d, 2 * PG_ROWS :] = jnp.concatenate([last, empty], axis=0).astype(out_ref.dtype)


def add_share_kernel(parts_ref, sent_in_ref, sent_ref, pieces, sem):
    total = parts_ref[0].astype(jnp.float32)
    for k in range(1, DP):
        total = total + parts_ref[k].astype(jnp.float32)
    for s in range(SHARDS):
        last = total[2 * PG_ROWS + s % 4 * PG_COLS :][:PG_COLS]
        last = last[:, s // 4 * 64 :][:, :64]
        blocks = [total[c * PG_ROWS + s * PG_COLS :][:PG_COLS] for c in range(2)]
        blocks.append(jnp.concatenate([last, jnp.zeros_like(last)], axis=1))
        for c, block in enumerate(blocks):
            block = jnp.concatenate([block, jnp.zeros((6, HALF), jnp.float32)], axis=0)
            pieces[s, 16 * c : 16 * (c + 1)] = block.astype(jnp.bfloat16)
    copy = pltpu.make_async_copy(pieces, sent_ref.at[:, pl.ds(PG_AT, OUT_ROWS - PG_AT)], sem)
    copy.start()
    copy.wait()


def grad_kernel(x_ref, *refs):
    near, (out_ref, *dq_refs) = refs[: len(NEAR)], refs[len(NEAR) : 2 * len(NEAR) + 1]
    k_t, v_t, dk, dv = refs[2 * len(NEAR) + 1 :]
    for s in range(SHARDS):
        for b in range(2):
            tokens = slice((2 * s + b) * HALF, (2 * s + b + 1) * HALF)
            k_t[:, tokens] = x_ref[s, K_AT + b * HD : K_AT + (b + 1) * HD]
            v_t[:HD, tokens] = x_ref[s, V_AT + b * HD : V_AT + (b + 1) * HD]
    row = lax.broadcasted_iota(jnp.int32, (EXT - HD, SHARDS * ROWS), 0)
    v_t[HD:] = jnp.where(row < 3, -1.0, 0.0).astype(jnp.bfloat16)
    for i, (block, dq_ref) in enumerate(zip(near, dq_refs)):
        q, g = block[:HD], block[HD:]
        scores = dot(q, k_t[...], TN)
        peak = jnp.max(scores, axis=1, keepdims=True) * (FACTOR * LOG2E)
        raised = jnp.exp2(scores * (FACTOR * LOG2E) - peak)
        prob = raised * (1.0 / jnp.sum(raised, axis=1, keepdims=True))
        shifted = dot(g, v_t[...], TN)
        dscore = (prob * shifted).astype(jnp.bfloat16)
        dv_part = dot(g[:HD], prob.astype(jnp.bfloat16), NN)
        dk_part = dot(q, dscore, NN)
        if i == 0:
            dv[...] = dv_part
            dk[...] = dk_part
        else:
            dv[...] += dv_part
            dk[...] += dk_part
        dq_ref[...] = (dot(k_t[...], dscore, NT) * FACTOR).astype(jnp.bfloat16)
    for s in range(SHARDS):
        for b in range(2):
            tokens = slice((2 * s + b) * HALF, (2 * s + b + 1) * HALF)
            at = b * HD
            out_ref[s, K_AT + at : K_AT + at + HD] = (dk[:, tokens] * FACTOR).astype(jnp.bfloat16)
            out_ref[s, V_AT + at : V_AT + at + HD] = dv[:, tokens].astype(jnp.bfloat16)


def unpack_kernel(x_ref, *refs):
    near, (dq_ref, dk_ref, dv_ref, pg_ref) = refs[: len(NEAR)], refs[len(NEAR) :]
    here = lax.axis_index("ctx")
    for away, ref in zip(NEAR, near):
        j = lax.rem(here + away, HEADS_HERE)
        dq_ref[pl.ds(pl.multiple_of(j * HD, 16), HD)] = ref[...]
    for j in range(HEADS_HERE):
        for ref, start in ((dk_ref, K_AT), (dv_ref, V_AT)):
            for b in range(2):
                rows = slice(start + b * HD, start + (b + 1) * HD)
                total = x_ref[j, rows].astype(jnp.float32)
                total = total + x_ref[HEADS_HERE + j, rows].astype(jnp.float32)
                total = total.astype(jnp.bfloat16)
                ref[j * HD : (j + 1) * HD, b * HALF : (b + 1) * HALF] = total
    total = x_ref[0, PG_AT:].astype(jnp.float32)
    for s in range(1, SHARDS):
        total = total + x_ref[s, PG_AT:].astype(jnp.float32)
    wide = jnp.concatenate([total[16 * c : 16 * (c + 1)] for c in range(3)], axis=1)
    pg_ref[...] = wide[:PG_COLS, :WIDE]


def call(kernel, outs, flops, transcendentals=0, scratch=(), mib=48, **more):
    return pl.pallas_call(
        kernel,
        out_shape=outs,
        scratch_shapes=scratch,
        compiler_params=pltpu.CompilerParams(vmem_limit_bytes=mib * 1024 * 1024),
        cost_estimate=pl.CostEstimate(
            flops=flops, bytes_accessed=2 * 1024 * 1024, transcendentals=transcendentals
        ),
        **more,
    )


def shifted_round(x, away):
    return lax.ppermute(x, "ctx", [(z, (z + away) % SHARDS) for z in range(SHARDS)])


def on_device(queries, keys, values, saved_out, cotangent, proj_weight):
    half, single = jnp.bfloat16, jnp.float32
    shape = jax.ShapeDtypeStruct
    vmem, anywhere = pl.BlockSpec(memory_space=pltpu.VMEM), pl.BlockSpec(memory_space=pl.ANY)
    whole = pltpu.VMEM((WIDE, ROWS), half)
    q, k, v, o, cot = (x.T for x in (queries, keys, values, saved_out, cotangent))

    pairs = call(
        pack_keys_kernel,
        shape((SHARDS, KV_ROWS, HALF), half),
        0,
        scratch=[whole] * 2 + [pltpu.SemaphoreType.DMA((2,))],
        in_specs=[anywhere] * 2,
        mib=60,
    )(k, v)
    pairs = lax.all_to_all(pairs, "ctx", 0, 0, tiled=True)

    full_cot = lax.all_gather(cot, "tp", axis=0, tiled=True)
    flops = 2 * ROWS * WIDE * 4 * WIDE
    *near, parts = call(
        pack_queries_and_proj_kernel,
        [shape((QG_ROWS, ROWS), half)] * len(NEAR) + [shape((DP, PG_USED, HALF), half)],
        2 * flops,
        scratch=[whole] * 3
        + [pltpu.VMEM((HEADS_HERE * (EXT - HD), ROWS), half), pltpu.SemaphoreType.DMA((2,))],
        in_specs=[anywhere] * 2 + [vmem] * 2,
        mib=48,
    )(q, o, full_cot, proj_weight)
    near = [near[0]] + [shifted_round(x, away) for away, x in zip(NEAR[1:], near[1:])]
    parts = lax.all_to_all(parts, "dp", 0, 0, tiled=True)

    tokens = SHARDS * ROWS
    sent, *dq = call(
        grad_kernel,
        [shape((SHARDS, OUT_ROWS, HALF), half)]
        + [shape((HD, ROWS), half)] * len(NEAR),
        5 * 2 * tokens * (tokens // 2) * HD,
        tokens * (tokens // 2),
        [
            pltpu.VMEM((HD, tokens), half),
            pltpu.VMEM((EXT, tokens), half),
            pltpu.VMEM((HD, tokens), single),
            pltpu.VMEM((HD, tokens), single),
        ],
    )(pairs, *near)
    sent = call(
        add_share_kernel,
        shape(sent.shape, half),
        0,
        scratch=[
            pltpu.VMEM((SHARDS, OUT_ROWS - PG_AT, HALF), half),
            pltpu.SemaphoreType.DMA,
        ],
        in_specs=[vmem, anywhere],
        out_specs=anywhere,
        input_output_aliases={1: 0},
    )(parts, sent)
    back = lax.all_to_all(sent, "ctx", 0, 0, tiled=True)
    dq = [dq[0]] + [shifted_round(x, -away) for away, x in zip(NEAR[1:], dq[1:])]
    grad = shape((WIDE, ROWS), half)
    outs = call(unpack_kernel, (grad, grad, grad, shape((PG_COLS, WIDE), single)), 0)(back, *dq)
    return tuple(x.T for x in outs)


def solution(mesh):
    rows = P(("dp", "ctx"), "tp")
    return jax.shard_map(
        on_device,
        mesh=mesh,
        in_specs=(rows, rows, rows, rows, rows, P("tp", None)),
        out_specs=(rows, rows, rows, P("tp", ("dp", "ctx"))),
        check_vma=False,
    )
```

```python
import math

import jax
import jax.numpy as jnp
from jax import lax
from jax.experimental import pallas as pl
from jax.experimental.pallas import tpu as pltpu
from jax.sharding import PartitionSpec as P

HD = 80
HEADS_HERE = 4
SHARDS = 8
DP = 16
ROWS = 256
HALF = 128
WIDE = HEADS_HERE * HD
FACTOR = HD ** (-0.5)
LOG2E = math.log2(math.e)
EXT = 96
QG_ROWS = HD + EXT
K_AT, V_AT, KV_ROWS = 0, 2 * HD, 4 * HD
PG_AT, OUT_ROWS = 4 * HD, 4 * HD + 32
PG_COLS = 10
PG_ROWS = 80
PG_USED = 208
NEAR = (0, 6, 1, 7)

NT = (((1,), (1,)), ((), ()))
TN = (((0,), (0,)), ((), ()))
NN = (((1,), (0,)), ((), ()))


def dot(left, right, dims):
    return lax.dot_general(left, right, dims, preferred_element_type=jnp.float32)


def pack_keys_kernel(k_hbm, v_hbm, out_ref, k_ref, v_ref, sems):
    pairs = ((k_hbm, k_ref), (v_hbm, v_ref))
    copies = [pltpu.make_async_copy(x, y, sems.at[i]) for i, (x, y) in enumerate(pairs)]
    for copy in copies:
        copy.start()
    for copy, ref, first in zip(copies, (k_ref, v_ref), (K_AT, V_AT)):
        copy.wait()
        for s in range(SHARDS):
            j = s % HEADS_HERE
            for b in range(2):
                at = first + b * HD
                out_ref[s, at : at + HD] = ref[j * HD : (j + 1) * HD, b * HALF : (b + 1) * HALF]


def pack_queries_kernel(q_hbm, o_hbm, cot_ref, w_ref, *refs):
    out_refs, (q_ref, o_ref, g_ref, extra_ref, sems) = refs[: len(NEAR)], refs[len(NEAR) :]
    pairs = ((q_hbm, q_ref), (o_hbm, o_ref))
    copies = [pltpu.make_async_copy(x, y, sems.at[i]) for i, (x, y) in enumerate(pairs)]
    for copy in copies:
        copy.start()
    g_ref[...] = dot(w_ref[...], cot_ref[...], NN).astype(jnp.bfloat16)
    for copy in copies:
        copy.wait()
    for j in range(HEADS_HERE):
        cols = slice(j * HD, (j + 1) * HD)
        delta = jnp.sum(
            g_ref[cols].astype(jnp.float32) * o_ref[cols].astype(jnp.float32),
            axis=0,
            keepdims=True,
        )
        high = delta.astype(jnp.bfloat16).astype(jnp.float32)
        rest = delta - high
        middle = rest.astype(jnp.bfloat16).astype(jnp.float32)
        low = rest - middle
        row = lax.broadcasted_iota(jnp.int32, (EXT - HD, ROWS), 0)
        extra = jnp.where(
            row == 0, high, jnp.where(row == 1, middle, jnp.where(row == 2, low, 0.0))
        )
        extra_ref[j * (EXT - HD) : (j + 1) * (EXT - HD)] = extra.astype(jnp.bfloat16)
    here = lax.axis_index("ctx")
    for away, ref in zip(NEAR, out_refs):
        j = lax.rem(here + away, HEADS_HERE)
        cols = pl.ds(pl.multiple_of(j * HD, 16), HD)
        ref[:HD] = q_ref[cols]
        ref[HD : 2 * HD] = g_ref[cols]
        rows = pl.ds(pl.multiple_of(j * (EXT - HD), 16), EXT - HD)
        ref[2 * HD :] = extra_ref[rows]


def proj_kernel(cot_ref, o_ref, kept_ref, given_ref):
    parity = lax.rem(lax.div(lax.axis_index("dp"), 2), 2)
    empty = jnp.zeros((PG_USED - 200, HALF), jnp.float32)
    for ref, wanted in ((given_ref, 1 - parity), (kept_ref, parity)):
        for k in range(SHARDS):
            d = (k // 2 * 2 + wanted) * 2 + k % 2
            start = pl.multiple_of(d * PG_ROWS, 16)
            part = dot(cot_ref[pl.ds(start, PG_ROWS)], o_ref[...], NT)
            for c in range(2):
                at = c * PG_ROWS
                ref[k, at : at + PG_ROWS] = part[:, HALF * c : HALF * (c + 1)].astype(ref.dtype)
            last = part[:, 2 * HALF :]
            last = jnp.concatenate([last[: PG_ROWS // 2], last[PG_ROWS // 2 :]], axis=1)
            ref[k, 2 * PG_ROWS :] = jnp.concatenate([last, empty], axis=0).astype(ref.dtype)


def add_kernel(kept_ref, taken_ref, out_ref):
    out_ref[...] = (kept_ref[...] + taken_ref[...].astype(jnp.float32)).astype(jnp.bfloat16)


def after_kernel(*refs):
    pass


def add_share_kernel(parts_ref, sent_in_ref, sent_ref, pieces, sem):
    total = parts_ref[0].astype(jnp.float32)
    for k in range(1, SHARDS):
        total = total + parts_ref[k].astype(jnp.float32)
    empty = jnp.zeros((1, HALF), jnp.float32)
    for s in range(SHARDS):
        blocks = [total[c * PG_ROWS + s * PG_COLS :][:PG_COLS] for c in range(2)]
        third = total[2 * PG_ROWS + s % 4 * PG_COLS :][:PG_COLS, s // 4 * 64 :][:, :64]
        blocks.append(jnp.concatenate([third[:5], third[5:]], axis=1))
        first = jnp.concatenate([blocks[0], blocks[2], empty], axis=0)
        second = jnp.concatenate([blocks[1], jnp.zeros((6, HALF), jnp.float32)], axis=0)
        pieces[s] = jnp.concatenate([first, second], axis=0).astype(jnp.bfloat16)
    copy = pltpu.make_async_copy(pieces, sent_ref.at[:, pl.ds(PG_AT, OUT_ROWS - PG_AT)], sem)
    copy.start()
    copy.wait()


def grad_kernel(x_ref, *refs):
    near, (out_ref, *dq_refs) = refs[: len(NEAR)], refs[len(NEAR) : 2 * len(NEAR) + 1]
    k_t, v_t, dk, dv = refs[2 * len(NEAR) + 1 :]
    for s in range(SHARDS):
        for b in range(2):
            tokens = slice((2 * s + b) * HALF, (2 * s + b + 1) * HALF)
            k_t[:, tokens] = x_ref[s, K_AT + b * HD : K_AT + (b + 1) * HD]
            v_t[:HD, tokens] = x_ref[s, V_AT + b * HD : V_AT + (b + 1) * HD]
    row = lax.broadcasted_iota(jnp.int32, (EXT - HD, SHARDS * ROWS), 0)
    v_t[HD:] = jnp.where(row < 3, -1.0, 0.0).astype(jnp.bfloat16)
    for i, (block, dq_ref) in enumerate(zip(near, dq_refs)):
        q, g = block[:HD], block[HD:]
        scores = dot(q, k_t[...], TN)
        peak = jnp.max(scores, axis=1, keepdims=True) * (FACTOR * LOG2E)
        raised = jnp.exp2(scores * (FACTOR * LOG2E) - peak)
        prob = raised * (1.0 / jnp.sum(raised, axis=1, keepdims=True))
        shifted = dot(g, v_t[...], TN)
        dscore = (prob * shifted).astype(jnp.bfloat16)
        dv_part = dot(g[:HD], prob.astype(jnp.bfloat16), NN)
        dk_part = dot(q, dscore, NN)
        if i == 0:
            dv[...] = dv_part
            dk[...] = dk_part
        else:
            dv[...] += dv_part
            dk[...] += dk_part
        dq_ref[...] = (dot(k_t[...], dscore, NT) * FACTOR).astype(jnp.bfloat16)
    for s in range(SHARDS):
        for b in range(2):
            tokens = slice((2 * s + b) * HALF, (2 * s + b + 1) * HALF)
            at = b * HD
            out_ref[s, K_AT + at : K_AT + at + HD] = (dk[:, tokens] * FACTOR).astype(jnp.bfloat16)
            out_ref[s, V_AT + at : V_AT + at + HD] = dv[:, tokens].astype(jnp.bfloat16)


def unpack_kernel(x_ref, *refs):
    near, (dq_ref, dk_ref, dv_ref, pg_ref) = refs[: len(NEAR)], refs[len(NEAR) :]
    here = lax.axis_index("ctx")
    for away, ref in zip(NEAR, near):
        j = lax.rem(here + away, HEADS_HERE)
        dq_ref[pl.ds(pl.multiple_of(j * HD, 16), HD)] = ref[...]
    for j in range(HEADS_HERE):
        for ref, start in ((dk_ref, K_AT), (dv_ref, V_AT)):
            for b in range(2):
                rows = slice(start + b * HD, start + (b + 1) * HD)
                total = x_ref[j, rows].astype(jnp.float32)
                total = total + x_ref[HEADS_HERE + j, rows].astype(jnp.float32)
                total = total.astype(jnp.bfloat16)
                ref[j * HD : (j + 1) * HD, b * HALF : (b + 1) * HALF] = total
    total = x_ref[0, PG_AT:].astype(jnp.float32)
    for s in range(1, SHARDS):
        total = total + x_ref[s, PG_AT:].astype(jnp.float32)
    last = total[PG_COLS : PG_COLS + 5]
    last = jnp.concatenate([last[:, :64], last[:, 64:]], axis=0)
    pg_ref[...] = jnp.concatenate([total[:PG_COLS], total[16 : 16 + PG_COLS], last], axis=1)


def call(kernel, outs, flops, transcendentals=0, scratch=(), mib=48, **more):
    return pl.pallas_call(
        kernel,
        out_shape=outs,
        scratch_shapes=scratch,
        compiler_params=pltpu.CompilerParams(vmem_limit_bytes=mib * 1024 * 1024),
        cost_estimate=pl.CostEstimate(
            flops=flops, bytes_accessed=2 * 1024 * 1024, transcendentals=transcendentals
        ),
        **more,
    )


def shifted_round(x, away):
    return lax.ppermute(x, "ctx", [(z, (z + away) % SHARDS) for z in range(SHARDS)])


def on_device(queries, keys, values, saved_out, cotangent, proj_weight):
    half, single = jnp.bfloat16, jnp.float32
    shape = jax.ShapeDtypeStruct
    vmem, anywhere = pl.BlockSpec(memory_space=pltpu.VMEM), pl.BlockSpec(memory_space=pl.ANY)
    whole = pltpu.VMEM((WIDE, ROWS), half)
    q, k, v, o, cot = (x.T for x in (queries, keys, values, saved_out, cotangent))

    pairs = call(
        pack_keys_kernel,
        shape((SHARDS, KV_ROWS, HALF), half),
        0,
        scratch=[whole] * 2 + [pltpu.SemaphoreType.DMA((2,))],
        in_specs=[anywhere] * 2,
        mib=60,
    )(k, v)
    pairs = lax.all_to_all(pairs, "ctx", 0, 0, tiled=True)

    full_cot = lax.all_gather(cot, "tp", axis=0, tiled=True)
    flops = 2 * ROWS * WIDE * 4 * WIDE
    block = (SHARDS, PG_USED, HALF)
    kept, given = call(proj_kernel, (shape(block, single), shape(block, half)), flops)(full_cot, o)
    taken = lax.ppermute(given, "dp", [(i, i ^ 2) for i in range(DP)])
    near = call(
        pack_queries_kernel,
        [shape((QG_ROWS, ROWS), half)] * len(NEAR),
        flops,
        scratch=[whole] * 3
        + [pltpu.VMEM((HEADS_HERE * (EXT - HD), ROWS), half), pltpu.SemaphoreType.DMA((2,))],
        in_specs=[anywhere] * 2 + [vmem] * 2,
        mib=48,
    )(q, o, full_cot, proj_weight)
    near = [near[0]] + [shifted_round(x, away) for away, x in zip(NEAR[1:], near[1:])]
    parts = call(add_kernel, shape(block, half), 0)(kept, taken)
    parts = call(
        after_kernel,
        shape(block, half),
        0,
        in_specs=[anywhere] * len(near),
        out_specs=anywhere,
        input_output_aliases={0: 0},
    )(parts, *near[1:])
    same_parity = [[(k // 2 * 2 + y) * 2 + k % 2 for k in range(SHARDS)] for y in range(2)]
    parts = lax.all_to_all(parts, "dp", 0, 0, tiled=True, axis_index_groups=same_parity)

    tokens = SHARDS * ROWS
    sent, *dq = call(
        grad_kernel,
        [shape((SHARDS, OUT_ROWS, HALF), half)]
        + [shape((HD, ROWS), half)] * len(NEAR),
        5 * 2 * tokens * (tokens // 2) * HD,
        tokens * (tokens // 2),
        [
            pltpu.VMEM((HD, tokens), half),
            pltpu.VMEM((EXT, tokens), half),
            pltpu.VMEM((HD, tokens), single),
            pltpu.VMEM((HD, tokens), single),
        ],
    )(pairs, *near)
    sent = call(
        add_share_kernel,
        shape(sent.shape, half),
        0,
        scratch=[
            pltpu.VMEM((SHARDS, OUT_ROWS - PG_AT, HALF), half),
            pltpu.SemaphoreType.DMA,
        ],
        in_specs=[vmem, anywhere],
        out_specs=anywhere,
        input_output_aliases={1: 0},
    )(parts, sent)
    back = lax.all_to_all(sent, "ctx", 0, 0, tiled=True)
    dq = [dq[0]] + [shifted_round(x, -away) for away, x in zip(NEAR[1:], dq[1:])]
    grad = shape((WIDE, ROWS), half)
    outs = call(unpack_kernel, (grad, grad, grad, shape((PG_COLS, WIDE), single)), 0)(back, *dq)
    return tuple(x.T for x in outs)


def solution(mesh):
    rows = P(("dp", "ctx"), "tp")
    return jax.shard_map(
        on_device,
        mesh=mesh,
        in_specs=(rows, rows, rows, rows, rows, P("tp", None)),
        out_specs=(rows, rows, rows, P("tp", ("dp", "ctx"))),
        check_vma=False,
    )
```

```python
import math

import jax
import jax.numpy as jnp
from jax import lax
from jax.experimental import pallas as pl
from jax.experimental.pallas import tpu as pltpu
from jax.sharding import PartitionSpec as P

HD = 80
HEADS_HERE = 4
SHARDS = 8
DP = 16
ROWS = 256
HALF = 128
WIDE = HEADS_HERE * HD
FACTOR = HD ** (-0.5)
LOG2E = math.log2(math.e)
EXT = 96
QG_ROWS = HD + EXT
K_AT, V_AT, KV_ROWS = 0, 2 * HD, 4 * HD
PG_AT, OUT_ROWS = 4 * HD, 4 * HD + 32
PG_COLS = 10
PG_ROWS = 80
PG_USED = 208
NEAR = (0, 2, 1, 7)

NT = (((1,), (1,)), ((), ()))
TN = (((0,), (0,)), ((), ()))
NN = (((1,), (0,)), ((), ()))


def dot(left, right, dims):
    return lax.dot_general(left, right, dims, preferred_element_type=jnp.float32)


def pack_keys_kernel(k_hbm, v_hbm, out_ref, k_ref, v_ref, sems):
    pairs = ((k_hbm, k_ref), (v_hbm, v_ref))
    copies = [pltpu.make_async_copy(x, y, sems.at[i]) for i, (x, y) in enumerate(pairs)]
    for copy in copies:
        copy.start()
    for copy, ref, first in zip(copies, (k_ref, v_ref), (K_AT, V_AT)):
        copy.wait()
        for s in range(SHARDS):
            j = s % HEADS_HERE
            for b in range(2):
                at = first + b * HD
                out_ref[s, at : at + HD] = ref[j * HD : (j + 1) * HD, b * HALF : (b + 1) * HALF]


def pack_queries_kernel(q_hbm, o_hbm, cot_ref, w_ref, *refs):
    out_refs, (q_ref, o_ref, g_ref, extra_ref, sems) = refs[: len(NEAR)], refs[len(NEAR) :]
    pairs = ((q_hbm, q_ref), (o_hbm, o_ref))
    copies = [pltpu.make_async_copy(x, y, sems.at[i]) for i, (x, y) in enumerate(pairs)]
    for copy in copies:
        copy.start()
    g_ref[...] = dot(w_ref[...], cot_ref[...], NN).astype(jnp.bfloat16)
    for copy in copies:
        copy.wait()
    for j in range(HEADS_HERE):
        cols = slice(j * HD, (j + 1) * HD)
        delta = jnp.sum(
            g_ref[cols].astype(jnp.float32) * o_ref[cols].astype(jnp.float32),
            axis=0,
            keepdims=True,
        )
        high = delta.astype(jnp.bfloat16).astype(jnp.float32)
        rest = delta - high
        middle = rest.astype(jnp.bfloat16).astype(jnp.float32)
        low = rest - middle
        row = lax.broadcasted_iota(jnp.int32, (EXT - HD, ROWS), 0)
        extra = jnp.where(
            row == 0, high, jnp.where(row == 1, middle, jnp.where(row == 2, low, 0.0))
        )
        extra_ref[j * (EXT - HD) : (j + 1) * (EXT - HD)] = extra.astype(jnp.bfloat16)
    here = lax.axis_index("ctx")
    for away, ref in zip(NEAR, out_refs):
        j = lax.rem(here + away, HEADS_HERE)
        cols = pl.ds(pl.multiple_of(j * HD, 16), HD)
        ref[:HD] = q_ref[cols]
        ref[HD : 2 * HD] = g_ref[cols]
        rows = pl.ds(pl.multiple_of(j * (EXT - HD), 16), EXT - HD)
        ref[2 * HD :] = extra_ref[rows]


def proj_kernel(cot_ref, o_ref, kept_ref, given_ref):
    upper = lax.rem(lax.axis_index("dp"), 2)
    empty = jnp.zeros((PG_USED - 200, HALF), jnp.float32)
    for ref, wanted in ((given_ref, 1 - upper), (kept_ref, upper)):
        for k in range(SHARDS):
            d = 2 * k + wanted
            start = pl.multiple_of(d * PG_ROWS, 16)
            part = dot(cot_ref[pl.ds(start, PG_ROWS)], o_ref[...], NT)
            for c in range(2):
                at = c * PG_ROWS
                ref[k, at : at + PG_ROWS] = part[:, HALF * c : HALF * (c + 1)].astype(ref.dtype)
            last = part[:, 2 * HALF :]
            last = jnp.concatenate([last[: PG_ROWS // 2], last[PG_ROWS // 2 :]], axis=1)
            ref[k, 2 * PG_ROWS :] = jnp.concatenate([last, empty], axis=0).astype(ref.dtype)


def add_kernel(kept_ref, taken_ref, out_ref):
    out_ref[...] = (kept_ref[...] + taken_ref[...].astype(jnp.float32)).astype(jnp.bfloat16)


def after_kernel(*refs):
    pass


def add_share_kernel(parts_ref, sent_in_ref, sent_ref, pieces, sem):
    total = parts_ref[0].astype(jnp.float32)
    for k in range(1, SHARDS):
        total = total + parts_ref[k].astype(jnp.float32)
    empty = jnp.zeros((1, HALF), jnp.float32)
    for s in range(SHARDS):
        blocks = [total[c * PG_ROWS + s * PG_COLS :][:PG_COLS] for c in range(2)]
        third = total[2 * PG_ROWS + s % 4 * PG_COLS :][:PG_COLS, s // 4 * 64 :][:, :64]
        blocks.append(jnp.concatenate([third[:5], third[5:]], axis=1))
        first = jnp.concatenate([blocks[0], blocks[2], empty], axis=0)
        second = jnp.concatenate([blocks[1], jnp.zeros((6, HALF), jnp.float32)], axis=0)
        pieces[s] = jnp.concatenate([first, second], axis=0).astype(jnp.bfloat16)
    copy = pltpu.make_async_copy(pieces, sent_ref.at[:, pl.ds(PG_AT, OUT_ROWS - PG_AT)], sem)
    copy.start()
    copy.wait()


def grad_kernel(x_ref, *refs):
    near, (out_ref, *dq_refs) = refs[: len(NEAR)], refs[len(NEAR) : 2 * len(NEAR) + 1]
    k_t, v_t, dk, dv = refs[2 * len(NEAR) + 1 :]
    for s in range(SHARDS):
        for b in range(2):
            tokens = slice((2 * s + b) * HALF, (2 * s + b + 1) * HALF)
            k_t[:, tokens] = x_ref[s, K_AT + b * HD : K_AT + (b + 1) * HD]
            v_t[:HD, tokens] = x_ref[s, V_AT + b * HD : V_AT + (b + 1) * HD]
    row = lax.broadcasted_iota(jnp.int32, (EXT - HD, SHARDS * ROWS), 0)
    v_t[HD:] = jnp.where(row < 3, -1.0, 0.0).astype(jnp.bfloat16)
    for i, (block, dq_ref) in enumerate(zip(near, dq_refs)):
        q, g = block[:HD], block[HD:]
        scores = dot(q, k_t[...], TN)
        peak = jnp.max(scores, axis=1, keepdims=True) * (FACTOR * LOG2E)
        raised = jnp.exp2(scores * (FACTOR * LOG2E) - peak)
        prob = raised * (1.0 / jnp.sum(raised, axis=1, keepdims=True))
        shifted = dot(g, v_t[...], TN)
        dscore = (prob * shifted).astype(jnp.bfloat16)
        dv_part = dot(g[:HD], prob.astype(jnp.bfloat16), NN)
        dk_part = dot(q, dscore, NN)
        if i == 0:
            dv[...] = dv_part
            dk[...] = dk_part
        else:
            dv[...] += dv_part
            dk[...] += dk_part
        dq_ref[...] = (dot(k_t[...], dscore, NT) * FACTOR).astype(jnp.bfloat16)
    for s in range(SHARDS):
        for b in range(2):
            tokens = slice((2 * s + b) * HALF, (2 * s + b + 1) * HALF)
            at = b * HD
            out_ref[s, K_AT + at : K_AT + at + HD] = (dk[:, tokens] * FACTOR).astype(jnp.bfloat16)
            out_ref[s, V_AT + at : V_AT + at + HD] = dv[:, tokens].astype(jnp.bfloat16)


def unpack_kernel(x_ref, *refs):
    near, (dq_ref, dk_ref, dv_ref, pg_ref) = refs[: len(NEAR)], refs[len(NEAR) :]
    here = lax.axis_index("ctx")
    for away, ref in zip(NEAR, near):
        j = lax.rem(here + away, HEADS_HERE)
        dq_ref[pl.ds(pl.multiple_of(j * HD, 16), HD)] = ref[...]
    for j in range(HEADS_HERE):
        for ref, start in ((dk_ref, K_AT), (dv_ref, V_AT)):
            for b in range(2):
                rows = slice(start + b * HD, start + (b + 1) * HD)
                total = x_ref[j, rows].astype(jnp.float32)
                total = total + x_ref[HEADS_HERE + j, rows].astype(jnp.float32)
                total = total.astype(jnp.bfloat16)
                ref[j * HD : (j + 1) * HD, b * HALF : (b + 1) * HALF] = total
    total = x_ref[0, PG_AT:].astype(jnp.float32)
    for s in range(1, SHARDS):
        total = total + x_ref[s, PG_AT:].astype(jnp.float32)
    last = total[PG_COLS : PG_COLS + 5]
    last = jnp.concatenate([last[:, :64], last[:, 64:]], axis=0)
    pg_ref[...] = jnp.concatenate([total[:PG_COLS], total[16 : 16 + PG_COLS], last], axis=1)


def call(kernel, outs, flops, transcendentals=0, scratch=(), mib=48, **more):
    return pl.pallas_call(
        kernel,
        out_shape=outs,
        scratch_shapes=scratch,
        compiler_params=pltpu.CompilerParams(vmem_limit_bytes=mib * 1024 * 1024),
        cost_estimate=pl.CostEstimate(
            flops=flops, bytes_accessed=2 * 1024 * 1024, transcendentals=transcendentals
        ),
        **more,
    )


def shifted_round(x, away, back=False):
    pairs = [
        (z, (z - away if away == 2 and z % 2 == 0 else z + away) % SHARDS) for z in range(SHARDS)
    ]
    return lax.ppermute(x, "ctx", [pair[::-1] for pair in pairs] if back else pairs)


def on_device(queries, keys, values, saved_out, cotangent, proj_weight):
    half, single = jnp.bfloat16, jnp.float32
    shape = jax.ShapeDtypeStruct
    vmem, anywhere = pl.BlockSpec(memory_space=pltpu.VMEM), pl.BlockSpec(memory_space=pl.ANY)
    whole = pltpu.VMEM((WIDE, ROWS), half)
    q, k, v, o, cot = (x.T for x in (queries, keys, values, saved_out, cotangent))

    pairs = call(
        pack_keys_kernel,
        shape((SHARDS, KV_ROWS, HALF), half),
        0,
        scratch=[whole] * 2 + [pltpu.SemaphoreType.DMA((2,))],
        in_specs=[anywhere] * 2,
        mib=60,
    )(k, v)
    pairs = lax.all_to_all(pairs, "ctx", 0, 0, tiled=True)

    full_cot = lax.all_gather(cot, "tp", axis=0, tiled=True)
    flops = 2 * ROWS * WIDE * 4 * WIDE
    block = (SHARDS, PG_USED, HALF)
    kept, given = call(proj_kernel, (shape(block, single), shape(block, half)), flops)(full_cot, o)
    taken = lax.ppermute(given, "dp", [(i, i ^ 1) for i in range(DP)])
    near = call(
        pack_queries_kernel,
        [shape((QG_ROWS, ROWS), half)] * len(NEAR),
        flops,
        scratch=[whole] * 3
        + [pltpu.VMEM((HEADS_HERE * (EXT - HD), ROWS), half), pltpu.SemaphoreType.DMA((2,))],
        in_specs=[anywhere] * 2 + [vmem] * 2,
        mib=48,
    )(q, o, full_cot, proj_weight)
    near = [near[0]] + [shifted_round(x, away) for away, x in zip(NEAR[1:], near[1:])]
    parts = call(add_kernel, shape(block, half), 0)(kept, taken)
    parts = call(
        after_kernel,
        shape(block, half),
        0,
        in_specs=[anywhere] * len(near),
        out_specs=anywhere,
        input_output_aliases={0: 0},
    )(parts, *near[1:])
    along_y = [list(range(x, DP, 2)) for x in range(2)]
    parts = lax.all_to_all(parts, "dp", 0, 0, tiled=True, axis_index_groups=along_y)

    tokens = SHARDS * ROWS
    sent, *dq = call(
        grad_kernel,
        [shape((SHARDS, OUT_ROWS, HALF), half)]
        + [shape((HD, ROWS), half)] * len(NEAR),
        5 * 2 * tokens * (tokens // 2) * HD,
        tokens * (tokens // 2),
        [
            pltpu.VMEM((HD, tokens), half),
            pltpu.VMEM((EXT, tokens), half),
            pltpu.VMEM((HD, tokens), single),
            pltpu.VMEM((HD, tokens), single),
        ],
    )(pairs, *near)
    sent = call(
        add_share_kernel,
        shape(sent.shape, half),
        0,
        scratch=[
            pltpu.VMEM((SHARDS, OUT_ROWS - PG_AT, HALF), half),
            pltpu.SemaphoreType.DMA,
        ],
        in_specs=[vmem, anywhere],
        out_specs=anywhere,
        input_output_aliases={1: 0},
    )(parts, sent)
    back = lax.all_to_all(sent, "ctx", 0, 0, tiled=True)
    dq = [dq[0]] + [shifted_round(x, away, back=True) for away, x in zip(NEAR[1:], dq[1:])]
    grad = shape((WIDE, ROWS), half)
    outs = call(unpack_kernel, (grad, grad, grad, shape((PG_COLS, WIDE), single)), 0)(back, *dq)
    return tuple(x.T for x in outs)


def solution(mesh):
    rows = P(("dp", "ctx"), "tp")
    return jax.shard_map(
        on_device,
        mesh=mesh,
        in_specs=(rows, rows, rows, rows, rows, P("tp", None)),
        out_specs=(rows, rows, rows, P("tp", ("dp", "ctx"))),
        check_vma=False,
    )
```

```python
import math

import jax
import jax.numpy as jnp
from jax import lax
from jax.experimental import pallas as pl
from jax.experimental.pallas import tpu as pltpu
from jax.sharding import PartitionSpec as P

HD = 80
HEADS_HERE = 4
SHARDS = 8
DP = 16
ROWS = 256
HALF = 128
WIDE = HEADS_HERE * HD
FACTOR = HD ** (-0.5)
LOG2E = math.log2(math.e)
EXT = 96
QG_ROWS = HD + EXT
K_AT, V_AT, KV_ROWS = 0, 2 * HD, 4 * HD
PG_AT, OUT_ROWS = 4 * HD, 4 * HD + 32
PG_COLS = 10
PG_ROWS = 80
PG_USED = 208
NEAR = (0, 2, 1, 7)

NT = (((1,), (1,)), ((), ()))
TN = (((0,), (0,)), ((), ()))
NN = (((1,), (0,)), ((), ()))


def dot(left, right, dims):
    return lax.dot_general(left, right, dims, preferred_element_type=jnp.float32)


def pack_keys_kernel(k_hbm, v_hbm, out_hbm, k_ref, v_ref, out_ref, in_sems, out_sems):
    arrays = ((k_hbm, k_ref, K_AT), (v_hbm, v_ref, V_AT))
    loads = []
    for j in range(HEADS_HERE):
        cols = pl.ds(j * HD, HD)
        for i, (hbm, ref, _) in enumerate(arrays):
            load = pltpu.make_async_copy(hbm.at[cols], ref.at[cols], in_sems.at[j, i])
            load.start()
            loads.append(load)
    stores = []
    for j in range(HEADS_HERE):
        for i, (_, ref, first) in enumerate(arrays):
            loads[2 * j + i].wait()
            for b in range(2):
                at = first + b * HD
                block = ref[j * HD : (j + 1) * HD, b * HALF : (b + 1) * HALF]
                out_ref[j, at : at + HD] = block
        for h in range(2):
            there = h * HEADS_HERE + j
            store = pltpu.make_async_copy(out_ref.at[j], out_hbm.at[there], out_sems.at[there])
            store.start()
            stores.append(store)
    for store in stores:
        store.wait()


def pack_queries_kernel(q_hbm, o_hbm, cot_ref, w_ref, *refs):
    out_refs, (q_ref, o_ref, g_ref, extra_ref, sems) = refs[: len(NEAR)], refs[len(NEAR) :]
    pairs = ((q_hbm, q_ref), (o_hbm, o_ref))
    copies = [pltpu.make_async_copy(x, y, sems.at[i]) for i, (x, y) in enumerate(pairs)]
    for copy in copies:
        copy.start()
    g_ref[...] = dot(w_ref[...], cot_ref[...], NN).astype(jnp.bfloat16)
    for copy in copies:
        copy.wait()
    for j in range(HEADS_HERE):
        cols = slice(j * HD, (j + 1) * HD)
        delta = jnp.sum(
            g_ref[cols].astype(jnp.float32) * o_ref[cols].astype(jnp.float32),
            axis=0,
            keepdims=True,
        )
        high = delta.astype(jnp.bfloat16).astype(jnp.float32)
        rest = delta - high
        middle = rest.astype(jnp.bfloat16).astype(jnp.float32)
        low = rest - middle
        row = lax.broadcasted_iota(jnp.int32, (EXT - HD, ROWS), 0)
        extra = jnp.where(
            row == 0, high, jnp.where(row == 1, middle, jnp.where(row == 2, low, 0.0))
        )
        extra_ref[j * (EXT - HD) : (j + 1) * (EXT - HD)] = extra.astype(jnp.bfloat16)
    here = lax.axis_index("ctx")
    for away, ref in zip(NEAR, out_refs):
        j = lax.rem(here + away, HEADS_HERE)
        cols = pl.ds(pl.multiple_of(j * HD, 16), HD)
        ref[:HD] = q_ref[cols]
        ref[HD : 2 * HD] = g_ref[cols]
        rows = pl.ds(pl.multiple_of(j * (EXT - HD), 16), EXT - HD)
        ref[2 * HD :] = extra_ref[rows]


def proj_kernel(cot_ref, o_ref, kept_ref, given_ref, term_ref):
    upper = lax.rem(lax.axis_index("dp"), 2)
    empty = jnp.zeros((PG_USED - 200, HALF), jnp.float32)
    term_ref[...] = dot(cot_ref[...], o_ref[...], NT)
    for ref, wanted in ((given_ref, 1 - upper), (kept_ref, upper)):
        for k in range(SHARDS):
            start = pl.multiple_of((2 * k + wanted) * PG_ROWS, 8)
            part = term_ref[pl.ds(start, PG_ROWS)]
            for c in range(2):
                at = c * PG_ROWS
                ref[k, at : at + PG_ROWS] = part[:, HALF * c : HALF * (c + 1)].astype(ref.dtype)
            last = part[:, 2 * HALF :]
            last = jnp.concatenate([last[: PG_ROWS // 2], last[PG_ROWS // 2 :]], axis=1)
            ref[k, 2 * PG_ROWS :] = jnp.concatenate([last, empty], axis=0).astype(ref.dtype)


def add_kernel(kept_ref, taken_ref, out_ref):
    out_ref[...] = (kept_ref[...] + taken_ref[...].astype(jnp.float32)).astype(jnp.bfloat16)


def after_kernel(*refs):
    pass


def add_share_kernel(parts_ref, sent_in_ref, sent_ref, pieces, sem):
    total = parts_ref[0].astype(jnp.float32)
    for k in range(1, SHARDS):
        total = total + parts_ref[k].astype(jnp.float32)
    empty = jnp.zeros((1, HALF), jnp.float32)
    for s in range(SHARDS):
        blocks = [total[c * PG_ROWS + s * PG_COLS :][:PG_COLS] for c in range(2)]
        third = total[2 * PG_ROWS + s % 4 * PG_COLS :][:PG_COLS, s // 4 * 64 :][:, :64]
        blocks.append(jnp.concatenate([third[:5], third[5:]], axis=1))
        first = jnp.concatenate([blocks[0], blocks[2], empty], axis=0)
        second = jnp.concatenate([blocks[1], jnp.zeros((6, HALF), jnp.float32)], axis=0)
        pieces[s] = jnp.concatenate([first, second], axis=0).astype(jnp.bfloat16)
    copy = pltpu.make_async_copy(pieces, sent_ref.at[:, pl.ds(PG_AT, OUT_ROWS - PG_AT)], sem)
    copy.start()
    copy.wait()


def grad_kernel(x_ref, *refs):
    near, (out_ref, *dq_refs) = refs[: len(NEAR)], refs[len(NEAR) : 2 * len(NEAR) + 1]
    k_t, v_t, dk, dv = refs[2 * len(NEAR) + 1 :]
    for s in range(SHARDS):
        for b in range(2):
            tokens = slice((2 * s + b) * HALF, (2 * s + b + 1) * HALF)
            k_t[:, tokens] = x_ref[s, K_AT + b * HD : K_AT + (b + 1) * HD]
            v_t[:HD, tokens] = x_ref[s, V_AT + b * HD : V_AT + (b + 1) * HD]
    row = lax.broadcasted_iota(jnp.int32, (EXT - HD, SHARDS * ROWS), 0)
    v_t[HD:] = jnp.where(row < 3, -1.0, 0.0).astype(jnp.bfloat16)
    for i, (block, dq_ref) in enumerate(zip(near, dq_refs)):
        q, g = block[:HD], block[HD:]
        scores = dot(q, k_t[...], TN)
        peak = jnp.max(scores, axis=1, keepdims=True) * (FACTOR * LOG2E)
        raised = jnp.exp2(scores * (FACTOR * LOG2E) - peak)
        prob = raised * (1.0 / jnp.sum(raised, axis=1, keepdims=True))
        shifted = dot(g, v_t[...], TN)
        dscore = (prob * shifted).astype(jnp.bfloat16)
        dv_part = dot(g[:HD], prob.astype(jnp.bfloat16), NN)
        dk_part = dot(q, dscore, NN)
        if i == 0:
            dv[...] = dv_part
            dk[...] = dk_part
        else:
            dv[...] += dv_part
            dk[...] += dk_part
        dq_ref[...] = (dot(k_t[...], dscore, NT) * FACTOR).astype(jnp.bfloat16)
    for s in range(SHARDS):
        for b in range(2):
            tokens = slice((2 * s + b) * HALF, (2 * s + b + 1) * HALF)
            at = b * HD
            out_ref[s, K_AT + at : K_AT + at + HD] = (dk[:, tokens] * FACTOR).astype(jnp.bfloat16)
            out_ref[s, V_AT + at : V_AT + at + HD] = dv[:, tokens].astype(jnp.bfloat16)


def unpack_kernel(x_ref, *refs):
    near, (dq_ref, dk_ref, dv_ref, pg_ref) = refs[: len(NEAR)], refs[len(NEAR) :]
    here = lax.axis_index("ctx")
    for away, ref in zip(NEAR, near):
        j = lax.rem(here + away, HEADS_HERE)
        dq_ref[pl.ds(pl.multiple_of(j * HD, 16), HD)] = ref[...]
    for j in range(HEADS_HERE):
        for ref, start in ((dk_ref, K_AT), (dv_ref, V_AT)):
            for b in range(2):
                rows = slice(start + b * HD, start + (b + 1) * HD)
                total = x_ref[j, rows].astype(jnp.float32)
                total = total + x_ref[HEADS_HERE + j, rows].astype(jnp.float32)
                total = total.astype(jnp.bfloat16)
                ref[j * HD : (j + 1) * HD, b * HALF : (b + 1) * HALF] = total
    total = x_ref[0, PG_AT:].astype(jnp.float32)
    for s in range(1, SHARDS):
        total = total + x_ref[s, PG_AT:].astype(jnp.float32)
    last = total[PG_COLS : PG_COLS + 5]
    last = jnp.concatenate([last[:, :64], last[:, 64:]], axis=0)
    pg_ref[...] = jnp.concatenate([total[:PG_COLS], total[16 : 16 + PG_COLS], last], axis=1)


def call(kernel, outs, flops, transcendentals=0, scratch=(), mib=48, **more):
    return pl.pallas_call(
        kernel,
        out_shape=outs,
        scratch_shapes=scratch,
        compiler_params=pltpu.CompilerParams(vmem_limit_bytes=mib * 1024 * 1024),
        cost_estimate=pl.CostEstimate(
            flops=flops, bytes_accessed=2 * 1024 * 1024, transcendentals=transcendentals
        ),
        **more,
    )


def shifted_round(x, away, back=False):
    pairs = [
        (z, (z - away if away == 2 and z % 2 == 0 else z + away) % SHARDS) for z in range(SHARDS)
    ]
    return lax.ppermute(x, "ctx", [pair[::-1] for pair in pairs] if back else pairs)


def on_device(queries, keys, values, saved_out, cotangent, proj_weight):
    half, single = jnp.bfloat16, jnp.float32
    shape = jax.ShapeDtypeStruct
    vmem, anywhere = pl.BlockSpec(memory_space=pltpu.VMEM), pl.BlockSpec(memory_space=pl.ANY)
    whole = pltpu.VMEM((WIDE, ROWS), half)
    q, k, v, o, cot = (x.T for x in (queries, keys, values, saved_out, cotangent))

    pairs = call(
        pack_keys_kernel,
        shape((SHARDS, KV_ROWS, HALF), half),
        0,
        scratch=[whole] * 2
        + [
            pltpu.VMEM((HEADS_HERE, KV_ROWS, HALF), half),
            pltpu.SemaphoreType.DMA((HEADS_HERE, 2)),
            pltpu.SemaphoreType.DMA((SHARDS,)),
        ],
        in_specs=[anywhere] * 2,
        out_specs=anywhere,
        mib=60,
    )(k, v)
    pairs = lax.all_to_all(pairs, "ctx", 0, 0, tiled=True)

    full_cot = lax.all_gather(cot, "tp", axis=0, tiled=True)
    flops = 2 * ROWS * WIDE * 4 * WIDE
    block = (SHARDS, PG_USED, HALF)
    kept, given = call(
        proj_kernel,
        (shape(block, single), shape(block, half)),
        flops,
        scratch=[pltpu.VMEM((DP * PG_ROWS, WIDE), single)],
    )(full_cot, o)
    taken = lax.ppermute(given, "dp", [(i, i ^ 1) for i in range(DP)])
    near = call(
        pack_queries_kernel,
        [shape((QG_ROWS, ROWS), half)] * len(NEAR),
        flops,
        scratch=[whole] * 3
        + [pltpu.VMEM((HEADS_HERE * (EXT - HD), ROWS), half), pltpu.SemaphoreType.DMA((2,))],
        in_specs=[anywhere] * 2 + [vmem] * 2,
        mib=48,
    )(q, o, full_cot, proj_weight)
    near = [near[0]] + [shifted_round(x, away) for away, x in zip(NEAR[1:], near[1:])]
    parts = call(add_kernel, shape(block, half), 0)(kept, taken)
    parts = call(
        after_kernel,
        shape(block, half),
        0,
        in_specs=[anywhere] * len(near),
        out_specs=anywhere,
        input_output_aliases={0: 0},
    )(parts, *near[1:])
    along_y = [list(range(x, DP, 2)) for x in range(2)]
    parts = lax.all_to_all(parts, "dp", 0, 0, tiled=True, axis_index_groups=along_y)

    tokens = SHARDS * ROWS
    sent, *dq = call(
        grad_kernel,
        [shape((SHARDS, OUT_ROWS, HALF), half)]
        + [shape((HD, ROWS), half)] * len(NEAR),
        5 * 2 * tokens * (tokens // 2) * HD,
        tokens * (tokens // 2),
        [
            pltpu.VMEM((HD, tokens), half),
            pltpu.VMEM((EXT, tokens), half),
            pltpu.VMEM((HD, tokens), single),
            pltpu.VMEM((HD, tokens), single),
        ],
    )(pairs, *near)
    sent = call(
        add_share_kernel,
        shape(sent.shape, half),
        0,
        scratch=[
            pltpu.VMEM((SHARDS, OUT_ROWS - PG_AT, HALF), half),
            pltpu.SemaphoreType.DMA,
        ],
        in_specs=[vmem, anywhere],
        out_specs=anywhere,
        input_output_aliases={1: 0},
    )(parts, sent)
    back = lax.all_to_all(sent, "ctx", 0, 0, tiled=True)
    dq = [dq[0]] + [shifted_round(x, away, back=True) for away, x in zip(NEAR[1:], dq[1:])]
    grad = shape((WIDE, ROWS), half)
    outs = call(unpack_kernel, (grad, grad, grad, shape((PG_COLS, WIDE), single)), 0)(back, *dq)
    return tuple(x.T for x in outs)


def solution(mesh):
    rows = P(("dp", "ctx"), "tp")
    return jax.shard_map(
        on_device,
        mesh=mesh,
        in_specs=(rows, rows, rows, rows, rows, P("tp", None)),
        out_specs=(rows, rows, rows, P("tp", ("dp", "ctx"))),
        check_vma=False,
    )
```

```python
import math

import jax
import jax.numpy as jnp
from jax import lax
from jax.experimental import pallas as pl
from jax.experimental.pallas import tpu as pltpu
from jax.sharding import PartitionSpec as P

HD = 80
HEADS_HERE = 4
SHARDS = 8
DP = 16
ROWS = 256
HALF = 128
WIDE = HEADS_HERE * HD
FACTOR = HD ** (-0.5)
LOG2E = math.log2(math.e)
EXT = 96
QG_ROWS = HD + EXT
K_AT, V_AT = 0, 2 * HD
PG_AT, OUT_ROWS = 4 * HD, 4 * HD + 32
PG_COLS = 10
PG_ROWS = 80
PG_USED = 208
NEAR = (0, 2, 1, 7)

NT = (((1,), (1,)), ((), ()))
TN = (((0,), (0,)), ((), ()))
NN = (((1,), (0,)), ((), ()))


def dot(left, right, dims):
    return lax.dot_general(left, right, dims, preferred_element_type=jnp.float32)


def pack_keys_kernel(k_hbm, v_hbm, out_hbm, k_ref, v_ref, in_sems, out_sems):
    arrays = ((k_hbm, k_ref), (v_hbm, v_ref))
    loads, stores = [], []
    for j in range(HEADS_HERE):
        cols = pl.ds(j * HD, HD)
        for i, (hbm, ref) in enumerate(arrays):
            load = pltpu.make_async_copy(hbm.at[cols], ref.at[cols], in_sems.at[j, i])
            load.start()
            loads.append(load)
    for j in range(HEADS_HERE):
        for i, (_, ref) in enumerate(arrays):
            loads[2 * j + i].wait()
            for h in range(2):
                there = h * HEADS_HERE + j
                store = pltpu.make_async_copy(
                    ref.at[pl.ds(j * HD, HD)],
                    out_hbm.at[there, pl.ds(i * HD, HD)],
                    out_sems.at[there, i],
                )
                store.start()
                stores.append(store)
    for store in stores:
        store.wait()


def pack_queries_kernel(q_hbm, o_hbm, cot_ref, w_ref, *refs):
    out_refs, (q_ref, o_ref, g_ref, extra_ref, sems) = refs[: len(NEAR)], refs[len(NEAR) :]
    pairs = ((q_hbm, q_ref), (o_hbm, o_ref))
    copies = [pltpu.make_async_copy(x, y, sems.at[i]) for i, (x, y) in enumerate(pairs)]
    for copy in copies:
        copy.start()
    g_ref[...] = dot(w_ref[...], cot_ref[...], NN).astype(jnp.bfloat16)
    for copy in copies:
        copy.wait()
    for j in range(HEADS_HERE):
        cols = slice(j * HD, (j + 1) * HD)
        delta = jnp.sum(
            g_ref[cols].astype(jnp.float32) * o_ref[cols].astype(jnp.float32),
            axis=0,
            keepdims=True,
        )
        high = delta.astype(jnp.bfloat16).astype(jnp.float32)
        rest = delta - high
        middle = rest.astype(jnp.bfloat16).astype(jnp.float32)
        low = rest - middle
        row = lax.broadcasted_iota(jnp.int32, (EXT - HD, ROWS), 0)
        extra = jnp.where(
            row == 0, high, jnp.where(row == 1, middle, jnp.where(row == 2, low, 0.0))
        )
        extra_ref[j * (EXT - HD) : (j + 1) * (EXT - HD)] = extra.astype(jnp.bfloat16)
    here = lax.axis_index("ctx")
    for away, ref in zip(NEAR, out_refs):
        j = lax.rem(here + away, HEADS_HERE)
        cols = pl.ds(pl.multiple_of(j * HD, 16), HD)
        ref[:HD] = q_ref[cols]
        ref[HD : 2 * HD] = g_ref[cols]
        rows = pl.ds(pl.multiple_of(j * (EXT - HD), 16), EXT - HD)
        ref[2 * HD :] = extra_ref[rows]


def proj_kernel(cot_ref, o_ref, kept_ref, given_ref, term_ref):
    upper = lax.rem(lax.axis_index("dp"), 2)
    empty = jnp.zeros((PG_USED - 200, HALF), jnp.float32)
    term_ref[...] = dot(cot_ref[...], o_ref[...], NT)
    for ref, wanted in ((given_ref, 1 - upper), (kept_ref, upper)):
        for k in range(SHARDS):
            start = pl.multiple_of((2 * k + wanted) * PG_ROWS, 8)
            part = term_ref[pl.ds(start, PG_ROWS)]
            for c in range(2):
                at = c * PG_ROWS
                ref[k, at : at + PG_ROWS] = part[:, HALF * c : HALF * (c + 1)].astype(ref.dtype)
            last = part[:, 2 * HALF :]
            last = jnp.concatenate([last[: PG_ROWS // 2], last[PG_ROWS // 2 :]], axis=1)
            ref[k, 2 * PG_ROWS :] = jnp.concatenate([last, empty], axis=0).astype(ref.dtype)


def add_kernel(kept_ref, taken_ref, out_ref):
    out_ref[...] = (kept_ref[...] + taken_ref[...].astype(jnp.float32)).astype(jnp.bfloat16)


def after_kernel(*refs):
    pass


def add_share_kernel(parts_ref, sent_in_ref, sent_ref, pieces, sem):
    total = parts_ref[0].astype(jnp.float32)
    for k in range(1, SHARDS):
        total = total + parts_ref[k].astype(jnp.float32)
    empty = jnp.zeros((1, HALF), jnp.float32)
    for s in range(SHARDS):
        blocks = [total[c * PG_ROWS + s * PG_COLS :][:PG_COLS] for c in range(2)]
        third = total[2 * PG_ROWS + s % 4 * PG_COLS :][:PG_COLS, s // 4 * 64 :][:, :64]
        blocks.append(jnp.concatenate([third[:5], third[5:]], axis=1))
        first = jnp.concatenate([blocks[0], blocks[2], empty], axis=0)
        second = jnp.concatenate([blocks[1], jnp.zeros((6, HALF), jnp.float32)], axis=0)
        pieces[s] = jnp.concatenate([first, second], axis=0).astype(jnp.bfloat16)
    copy = pltpu.make_async_copy(pieces, sent_ref.at[:, pl.ds(PG_AT, OUT_ROWS - PG_AT)], sem)
    copy.start()
    copy.wait()


def grad_kernel(x_ref, *refs):
    near, (out_ref, *dq_refs) = refs[: len(NEAR)], refs[len(NEAR) : 2 * len(NEAR) + 1]
    k_t, v_t, dk, dv = refs[2 * len(NEAR) + 1 :]
    for s in range(SHARDS):
        tokens = slice(s * ROWS, (s + 1) * ROWS)
        k_t[:, tokens] = x_ref[s, :HD]
        v_t[:HD, tokens] = x_ref[s, HD:]
    row = lax.broadcasted_iota(jnp.int32, (EXT - HD, SHARDS * ROWS), 0)
    v_t[HD:] = jnp.where(row < 3, -1.0, 0.0).astype(jnp.bfloat16)
    for i, (block, dq_ref) in enumerate(zip(near, dq_refs)):
        q, g = block[:HD], block[HD:]
        scores = dot(q, k_t[...], TN)
        peak = jnp.max(scores, axis=1, keepdims=True) * (FACTOR * LOG2E)
        raised = jnp.exp2(scores * (FACTOR * LOG2E) - peak)
        prob = raised * (1.0 / jnp.sum(raised, axis=1, keepdims=True))
        shifted = dot(g, v_t[...], TN)
        dscore = (prob * shifted).astype(jnp.bfloat16)
        dv_part = dot(g[:HD], prob.astype(jnp.bfloat16), NN)
        dk_part = dot(q, dscore, NN)
        if i == 0:
            dv[...] = dv_part
            dk[...] = dk_part
        else:
            dv[...] += dv_part
            dk[...] += dk_part
        dq_ref[...] = (dot(k_t[...], dscore, NT) * FACTOR).astype(jnp.bfloat16)
    for s in range(SHARDS):
        for b in range(2):
            tokens = slice((2 * s + b) * HALF, (2 * s + b + 1) * HALF)
            at = b * HD
            out_ref[s, K_AT + at : K_AT + at + HD] = (dk[:, tokens] * FACTOR).astype(jnp.bfloat16)
            out_ref[s, V_AT + at : V_AT + at + HD] = dv[:, tokens].astype(jnp.bfloat16)


def unpack_kernel(x_ref, *refs):
    near, (dq_ref, dk_ref, dv_ref, pg_ref) = refs[: len(NEAR)], refs[len(NEAR) :]
    here = lax.axis_index("ctx")
    for away, ref in zip(NEAR, near):
        j = lax.rem(here + away, HEADS_HERE)
        dq_ref[pl.ds(pl.multiple_of(j * HD, 16), HD)] = ref[...]
    for j in range(HEADS_HERE):
        for ref, start in ((dk_ref, K_AT), (dv_ref, V_AT)):
            for b in range(2):
                rows = slice(start + b * HD, start + (b + 1) * HD)
                total = x_ref[j, rows].astype(jnp.float32)
                total = total + x_ref[HEADS_HERE + j, rows].astype(jnp.float32)
                total = total.astype(jnp.bfloat16)
                ref[j * HD : (j + 1) * HD, b * HALF : (b + 1) * HALF] = total
    total = x_ref[0, PG_AT:].astype(jnp.float32)
    for s in range(1, SHARDS):
        total = total + x_ref[s, PG_AT:].astype(jnp.float32)
    last = total[PG_COLS : PG_COLS + 5]
    last = jnp.concatenate([last[:, :64], last[:, 64:]], axis=0)
    pg_ref[...] = jnp.concatenate([total[:PG_COLS], total[16 : 16 + PG_COLS], last], axis=1)


def call(kernel, outs, flops, transcendentals=0, scratch=(), mib=48, **more):
    return pl.pallas_call(
        kernel,
        out_shape=outs,
        scratch_shapes=scratch,
        compiler_params=pltpu.CompilerParams(vmem_limit_bytes=mib * 1024 * 1024),
        cost_estimate=pl.CostEstimate(
            flops=flops, bytes_accessed=2 * 1024 * 1024, transcendentals=transcendentals
        ),
        **more,
    )


def shifted_round(x, away, back=False):
    pairs = [
        (z, (z - away if away == 2 and z % 2 == 0 else z + away) % SHARDS) for z in range(SHARDS)
    ]
    return lax.ppermute(x, "ctx", [pair[::-1] for pair in pairs] if back else pairs)


def on_device(queries, keys, values, saved_out, cotangent, proj_weight):
    half, single = jnp.bfloat16, jnp.float32
    shape = jax.ShapeDtypeStruct
    vmem, anywhere = pl.BlockSpec(memory_space=pltpu.VMEM), pl.BlockSpec(memory_space=pl.ANY)
    whole = pltpu.VMEM((WIDE, ROWS), half)
    q, k, v, o, cot = (x.T for x in (queries, keys, values, saved_out, cotangent))

    pairs = call(
        pack_keys_kernel,
        shape((SHARDS, 2 * HD, ROWS), half),
        0,
        scratch=[whole] * 2
        + [pltpu.SemaphoreType.DMA((HEADS_HERE, 2)), pltpu.SemaphoreType.DMA((SHARDS, 2))],
        in_specs=[anywhere] * 2,
        out_specs=anywhere,
        mib=60,
    )(k, v)
    pairs = lax.all_to_all(pairs, "ctx", 0, 0, tiled=True)

    full_cot = lax.all_gather(cot, "tp", axis=0, tiled=True)
    flops = 2 * ROWS * WIDE * 4 * WIDE
    block = (SHARDS, PG_USED, HALF)
    kept, given = call(
        proj_kernel,
        (shape(block, single), shape(block, half)),
        flops,
        scratch=[pltpu.VMEM((DP * PG_ROWS, WIDE), single)],
    )(full_cot, o)
    taken = lax.ppermute(given, "dp", [(i, i ^ 1) for i in range(DP)])
    near = call(
        pack_queries_kernel,
        [shape((QG_ROWS, ROWS), half)] * len(NEAR),
        flops,
        scratch=[whole] * 3
        + [pltpu.VMEM((HEADS_HERE * (EXT - HD), ROWS), half), pltpu.SemaphoreType.DMA((2,))],
        in_specs=[anywhere] * 2 + [vmem] * 2,
        mib=48,
    )(q, o, full_cot, proj_weight)
    near = [near[0]] + [shifted_round(x, away) for away, x in zip(NEAR[1:], near[1:])]
    parts = call(add_kernel, shape(block, half), 0)(kept, taken)
    parts = call(
        after_kernel,
        shape(block, half),
        0,
        in_specs=[anywhere] * len(near),
        out_specs=anywhere,
        input_output_aliases={0: 0},
    )(parts, *near[1:])
    along_y = [list(range(x, DP, 2)) for x in range(2)]
    parts = lax.all_to_all(parts, "dp", 0, 0, tiled=True, axis_index_groups=along_y)

    tokens = SHARDS * ROWS
    sent, *dq = call(
        grad_kernel,
        [shape((SHARDS, OUT_ROWS, HALF), half)]
        + [shape((HD, ROWS), half)] * len(NEAR),
        5 * 2 * tokens * (tokens // 2) * HD,
        tokens * (tokens // 2),
        [
            pltpu.VMEM((HD, tokens), half),
            pltpu.VMEM((EXT, tokens), half),
            pltpu.VMEM((HD, tokens), single),
            pltpu.VMEM((HD, tokens), single),
        ],
    )(pairs, *near)
    sent = call(
        add_share_kernel,
        shape(sent.shape, half),
        0,
        scratch=[
            pltpu.VMEM((SHARDS, OUT_ROWS - PG_AT, HALF), half),
            pltpu.SemaphoreType.DMA,
        ],
        in_specs=[vmem, anywhere],
        out_specs=anywhere,
        input_output_aliases={1: 0},
    )(parts, sent)
    back = lax.all_to_all(sent, "ctx", 0, 0, tiled=True)
    dq = [dq[0]] + [shifted_round(x, away, back=True) for away, x in zip(NEAR[1:], dq[1:])]
    grad = shape((WIDE, ROWS), half)
    outs = call(unpack_kernel, (grad, grad, grad, shape((PG_COLS, WIDE), single)), 0)(back, *dq)
    return tuple(x.T for x in outs)


def solution(mesh):
    rows = P(("dp", "ctx"), "tp")
    return jax.shard_map(
        on_device,
        mesh=mesh,
        in_specs=(rows, rows, rows, rows, rows, P("tp", None)),
        out_specs=(rows, rows, rows, P("tp", ("dp", "ctx"))),
        check_vma=False,
    )
```

```python
import math

import jax
import jax.numpy as jnp
from jax import lax
from jax.experimental import pallas as pl
from jax.experimental.pallas import tpu as pltpu
from jax.sharding import PartitionSpec as P

HD = 80
HEADS_HERE = 4
SHARDS = 8
DP = 16
ROWS = 256
HALF = 128
WIDE = HEADS_HERE * HD
FACTOR = HD ** (-0.5)
LOG2E = math.log2(math.e)
EXT = 96
QG_ROWS = HD + EXT
K_AT, V_AT, KV_ROWS = 0, 2 * HD, 4 * HD
PG_AT, OUT_ROWS = 4 * HD, 4 * HD + 32
PG_COLS = 10
PG_ROWS = 80
PG_USED = 208
NEAR = (0, 2, 1, 7)

NT = (((1,), (1,)), ((), ()))
TN = (((0,), (0,)), ((), ()))
NN = (((1,), (0,)), ((), ()))


def dot(left, right, dims):
    return lax.dot_general(left, right, dims, preferred_element_type=jnp.float32)


def pack_keys_kernel(k_hbm, v_hbm, out_hbm, k_ref, v_ref, out_ref, in_sems, out_sems):
    arrays = ((k_hbm, k_ref, K_AT), (v_hbm, v_ref, V_AT))
    loads = []
    for j in range(HEADS_HERE):
        cols = pl.ds(j * HD, HD)
        for i, (hbm, ref, _) in enumerate(arrays):
            load = pltpu.make_async_copy(hbm.at[cols], ref.at[cols], in_sems.at[j, i])
            load.start()
            loads.append(load)
    stores = []
    for j in range(HEADS_HERE):
        for i, (_, ref, first) in enumerate(arrays):
            loads[2 * j + i].wait()
            for b in range(2):
                at = first + b * HD
                block = ref[j * HD : (j + 1) * HD, b * HALF : (b + 1) * HALF]
                out_ref[j, at : at + HD] = block
        for h in range(2):
            there = h * HEADS_HERE + j
            store = pltpu.make_async_copy(out_ref.at[j], out_hbm.at[there], out_sems.at[there])
            store.start()
            stores.append(store)
    for store in stores:
        store.wait()


def pack_queries_kernel(q_hbm, o_hbm, cot_ref, w_ref, *refs):
    out_refs, (q_ref, o_ref, g_ref, extra_ref, sems) = refs[: len(NEAR)], refs[len(NEAR) :]
    pairs = ((q_hbm, q_ref), (o_hbm, o_ref))
    copies = [pltpu.make_async_copy(x, y, sems.at[i]) for i, (x, y) in enumerate(pairs)]
    for copy in copies:
        copy.start()
    g_ref[...] = dot(w_ref[...], cot_ref[...], NN).astype(jnp.bfloat16)
    for copy in copies:
        copy.wait()
    for j in range(HEADS_HERE):
        cols = slice(j * HD, (j + 1) * HD)
        delta = jnp.sum(
            g_ref[cols].astype(jnp.float32) * o_ref[cols].astype(jnp.float32),
            axis=0,
            keepdims=True,
        )
        high = delta.astype(jnp.bfloat16).astype(jnp.float32)
        rest = delta - high
        middle = rest.astype(jnp.bfloat16).astype(jnp.float32)
        low = rest - middle
        row = lax.broadcasted_iota(jnp.int32, (EXT - HD, ROWS), 0)
        extra = jnp.where(
            row == 0, high, jnp.where(row == 1, middle, jnp.where(row == 2, low, 0.0))
        )
        extra_ref[j * (EXT - HD) : (j + 1) * (EXT - HD)] = extra.astype(jnp.bfloat16)
    here = lax.axis_index("ctx")
    for away, ref in zip(NEAR, out_refs):
        j = lax.rem(here + away, HEADS_HERE)
        cols = pl.ds(pl.multiple_of(j * HD, 16), HD)
        ref[:HD] = q_ref[cols]
        ref[HD : 2 * HD] = g_ref[cols]
        rows = pl.ds(pl.multiple_of(j * (EXT - HD), 16), EXT - HD)
        ref[2 * HD :] = extra_ref[rows]


def proj_kernel(cot_ref, o_ref, kept_ref, given_ref, term_ref):
    upper = lax.rem(lax.axis_index("dp"), 2)
    empty = jnp.zeros((PG_USED - 200, HALF), jnp.float32)
    term_ref[...] = dot(cot_ref[...], o_ref[...], NT)
    for ref, wanted in ((given_ref, 1 - upper), (kept_ref, upper)):
        for k in range(SHARDS):
            start = pl.multiple_of((2 * k + wanted) * PG_ROWS, 8)
            part = term_ref[pl.ds(start, PG_ROWS)]
            for c in range(2):
                at = c * PG_ROWS
                ref[k, at : at + PG_ROWS] = part[:, HALF * c : HALF * (c + 1)].astype(ref.dtype)
            last = part[:, 2 * HALF :]
            last = jnp.concatenate([last[: PG_ROWS // 2], last[PG_ROWS // 2 :]], axis=1)
            ref[k, 2 * PG_ROWS :] = jnp.concatenate([last, empty], axis=0).astype(ref.dtype)


def add_kernel(kept_ref, taken_ref, _, out_ref):
    out_ref[...] = (kept_ref[...] + taken_ref[...].astype(jnp.float32)).astype(jnp.bfloat16)


def after_kernel(*refs):
    pass


def add_share_kernel(parts_ref, sent_in_ref, sent_ref, pieces, sem):
    total = parts_ref[0].astype(jnp.float32)
    for k in range(1, SHARDS):
        total = total + parts_ref[k].astype(jnp.float32)
    empty = jnp.zeros((1, HALF), jnp.float32)
    for s in range(SHARDS):
        blocks = [total[c * PG_ROWS + s * PG_COLS :][:PG_COLS] for c in range(2)]
        third = total[2 * PG_ROWS + s % 4 * PG_COLS :][:PG_COLS, s // 4 * 64 :][:, :64]
        blocks.append(jnp.concatenate([third[:5], third[5:]], axis=1))
        first = jnp.concatenate([blocks[0], blocks[2], empty], axis=0)
        second = jnp.concatenate([blocks[1], jnp.zeros((6, HALF), jnp.float32)], axis=0)
        pieces[s] = jnp.concatenate([first, second], axis=0).astype(jnp.bfloat16)
    copy = pltpu.make_async_copy(pieces, sent_ref.at[:, pl.ds(PG_AT, OUT_ROWS - PG_AT)], sem)
    copy.start()
    copy.wait()


def grad_blocks(blocks, dq_refs, k_ref, v_ref, dk, dv):
    for block, dq_ref in zip(blocks, dq_refs):
        q, g = block[:HD], block[HD:]
        scores = dot(q, k_ref[...], TN)
        peak = jnp.max(scores, axis=1, keepdims=True) * (FACTOR * LOG2E)
        raised = jnp.exp2(scores * (FACTOR * LOG2E) - peak)
        prob = raised * (1.0 / jnp.sum(raised, axis=1, keepdims=True))
        shifted = dot(g, v_ref[...], TN)
        dscore = (prob * shifted).astype(jnp.bfloat16)
        dv_part = dot(g[:HD], prob.astype(jnp.bfloat16), NN)
        dk_part = dot(q, dscore, NN)
        dk = dk_part if dk is None else dk + dk_part
        dv = dv_part if dv is None else dv + dv_part
        dq_ref[...] = (dot(k_ref[...], dscore, NT) * FACTOR).astype(jnp.bfloat16)
    return dk, dv


def own_grad_kernel(x_ref, block_ref, k_ref, v_ref, dk_ref, dv_ref, dq_ref):
    for s in range(SHARDS):
        for b in range(2):
            tokens = slice((2 * s + b) * HALF, (2 * s + b + 1) * HALF)
            k_ref[:, tokens] = x_ref[s, K_AT + b * HD : K_AT + (b + 1) * HD]
            v_ref[:HD, tokens] = x_ref[s, V_AT + b * HD : V_AT + (b + 1) * HD]
    row = lax.broadcasted_iota(jnp.int32, (EXT - HD, SHARDS * ROWS), 0)
    v_ref[HD:] = jnp.where(row < 3, -1.0, 0.0).astype(jnp.bfloat16)
    dk_ref[...], dv_ref[...] = grad_blocks([block_ref], [dq_ref], k_ref, v_ref, None, None)


def near_grad_kernel(k_ref, v_ref, dk_in_ref, dv_in_ref, *refs):
    number = (len(refs) - 2) // 2
    blocks, (dk_ref, dv_ref), dq_refs = refs[:number], refs[number : number + 2], refs[-number:]
    dk_ref[...], dv_ref[...] = grad_blocks(
        blocks, dq_refs, k_ref, v_ref, dk_in_ref[...], dv_in_ref[...]
    )


def last_grad_kernel(k_ref, v_ref, dk_in_ref, dv_in_ref, block_ref, out_ref, dq_ref):
    dk, dv = grad_blocks([block_ref], [dq_ref], k_ref, v_ref, dk_in_ref[...], dv_in_ref[...])
    dk, dv = (dk * FACTOR).astype(jnp.bfloat16), dv.astype(jnp.bfloat16)
    for s in range(SHARDS):
        for b in range(2):
            tokens = slice((2 * s + b) * HALF, (2 * s + b + 1) * HALF)
            at = b * HD
            out_ref[s, K_AT + at : K_AT + at + HD] = dk[:, tokens]
            out_ref[s, V_AT + at : V_AT + at + HD] = dv[:, tokens]


def unpack_kernel(x_ref, *refs):
    near, (dq_ref, dk_ref, dv_ref, pg_ref) = refs[: len(NEAR)], refs[len(NEAR) :]
    here = lax.axis_index("ctx")
    for away, ref in zip(NEAR, near):
        j = lax.rem(here + away, HEADS_HERE)
        dq_ref[pl.ds(pl.multiple_of(j * HD, 16), HD)] = ref[...]
    for j in range(HEADS_HERE):
        for ref, start in ((dk_ref, K_AT), (dv_ref, V_AT)):
            for b in range(2):
                rows = slice(start + b * HD, start + (b + 1) * HD)
                total = x_ref[j, rows].astype(jnp.float32)
                total = total + x_ref[HEADS_HERE + j, rows].astype(jnp.float32)
                total = total.astype(jnp.bfloat16)
                ref[j * HD : (j + 1) * HD, b * HALF : (b + 1) * HALF] = total
    total = x_ref[0, PG_AT:].astype(jnp.float32)
    for s in range(1, SHARDS):
        total = total + x_ref[s, PG_AT:].astype(jnp.float32)
    last = total[PG_COLS : PG_COLS + 5]
    last = jnp.concatenate([last[:, :64], last[:, 64:]], axis=0)
    pg_ref[...] = jnp.concatenate([total[:PG_COLS], total[16 : 16 + PG_COLS], last], axis=1)


def call(kernel, outs, flops, transcendentals=0, scratch=(), mib=48, **more):
    return pl.pallas_call(
        kernel,
        out_shape=outs,
        scratch_shapes=scratch,
        compiler_params=pltpu.CompilerParams(vmem_limit_bytes=mib * 1024 * 1024),
        cost_estimate=pl.CostEstimate(
            flops=flops, bytes_accessed=2 * 1024 * 1024, transcendentals=transcendentals
        ),
        **more,
    )


def shifted_round(x, away, back=False):
    pairs = [
        (z, (z - away if away == 2 and z % 2 == 0 else z + away) % SHARDS) for z in range(SHARDS)
    ]
    return lax.ppermute(x, "ctx", [pair[::-1] for pair in pairs] if back else pairs)


def on_device(queries, keys, values, saved_out, cotangent, proj_weight):
    half, single = jnp.bfloat16, jnp.float32
    shape = jax.ShapeDtypeStruct
    vmem, anywhere = pl.BlockSpec(memory_space=pltpu.VMEM), pl.BlockSpec(memory_space=pl.ANY)
    whole = pltpu.VMEM((WIDE, ROWS), half)
    q, k, v, o, cot = (x.T for x in (queries, keys, values, saved_out, cotangent))

    pairs = call(
        pack_keys_kernel,
        shape((SHARDS, KV_ROWS, HALF), half),
        0,
        scratch=[whole] * 2
        + [
            pltpu.VMEM((HEADS_HERE, KV_ROWS, HALF), half),
            pltpu.SemaphoreType.DMA((HEADS_HERE, 2)),
            pltpu.SemaphoreType.DMA((SHARDS,)),
        ],
        in_specs=[anywhere] * 2,
        out_specs=anywhere,
        mib=60,
    )(k, v)
    pairs = lax.all_to_all(pairs, "ctx", 0, 0, tiled=True)

    full_cot = lax.all_gather(cot, "tp", axis=0, tiled=True)
    flops = 2 * ROWS * WIDE * 4 * WIDE
    block = (SHARDS, PG_USED, HALF)
    kept, given = call(
        proj_kernel,
        (shape(block, single), shape(block, half)),
        flops,
        scratch=[pltpu.VMEM((DP * PG_ROWS, WIDE), single)],
    )(full_cot, o)
    taken = lax.ppermute(given, "dp", [(i, i ^ 1) for i in range(DP)])
    near = call(
        pack_queries_kernel,
        [shape((QG_ROWS, ROWS), half)] * len(NEAR),
        flops,
        scratch=[whole] * 3
        + [pltpu.VMEM((HEADS_HERE * (EXT - HD), ROWS), half), pltpu.SemaphoreType.DMA((2,))],
        in_specs=[anywhere] * 2 + [vmem] * 2,
        mib=48,
    )(q, o, full_cot, proj_weight)
    near = [near[0]] + [shifted_round(x, away) for away, x in zip(NEAR[1:], near[1:])]
    tokens = SHARDS * ROWS
    sums = [shape((HD, tokens), single)] * 2
    grad = shape((HD, ROWS), half)
    cost = (5 * 2 * tokens * ROWS * HD, tokens * ROWS)
    both = [shape((HD, tokens), half), shape((EXT, tokens), half)]
    k_all, v_all, dk, dv, dq_own = call(own_grad_kernel, both + sums + [grad], *cost, mib=32)(
        pairs, near[0]
    )
    parts = call(
        add_kernel, shape(block, half), 0, in_specs=[vmem, vmem, anywhere]
    )(kept, taken, dq_own)
    parts = call(
        after_kernel,
        shape(block, half),
        0,
        in_specs=[anywhere] * 4,
        out_specs=anywhere,
        input_output_aliases={0: 0},
    )(parts, *near[1:3], dq_own)
    along_y = [list(range(x, DP, 2)) for x in range(2)]
    parts = lax.all_to_all(parts, "dp", 0, 0, tiled=True, axis_index_groups=along_y)

    dk, dv, *dq_near = call(
        near_grad_kernel, sums + [grad] * 2, 2 * cost[0], 2 * cost[1], mib=32
    )(k_all, v_all, dk, dv, *near[1:3])
    sent, dq_last = call(
        last_grad_kernel, [shape((SHARDS, OUT_ROWS, HALF), half), grad], *cost, mib=32
    )(k_all, v_all, dk, dv, near[3])
    dq = [dq_own, *dq_near, dq_last]
    sent = call(
        add_share_kernel,
        shape(sent.shape, half),
        0,
        scratch=[
            pltpu.VMEM((SHARDS, OUT_ROWS - PG_AT, HALF), half),
            pltpu.SemaphoreType.DMA,
        ],
        in_specs=[vmem, anywhere],
        out_specs=anywhere,
        input_output_aliases={1: 0},
    )(parts, sent)
    back = lax.all_to_all(sent, "ctx", 0, 0, tiled=True)
    dq = [dq[0]] + [shifted_round(x, away, back=True) for away, x in zip(NEAR[1:], dq[1:])]
    grad = shape((WIDE, ROWS), half)
    outs = call(unpack_kernel, (grad, grad, grad, shape((PG_COLS, WIDE), single)), 0)(back, *dq)
    return tuple(x.T for x in outs)


def solution(mesh):
    rows = P(("dp", "ctx"), "tp")
    return jax.shard_map(
        on_device,
        mesh=mesh,
        in_specs=(rows, rows, rows, rows, rows, P("tp", None)),
        out_specs=(rows, rows, rows, P("tp", ("dp", "ctx"))),
        check_vma=False,
    )
```

```python
import math

import jax
import jax.numpy as jnp
from jax import lax
from jax.experimental import pallas as pl
from jax.experimental.pallas import tpu as pltpu
from jax.sharding import PartitionSpec as P

HD = 80
HEADS_HERE = 4
SHARDS = 8
DP = 16
ROWS = 256
HALF = 128
WIDE = HEADS_HERE * HD
FACTOR = HD ** (-0.5)
LOG2E = math.log2(math.e)
EXT = 96
QG_ROWS = HD + EXT
K_AT, V_AT, KV_ROWS = 0, 2 * HD, 4 * HD
PG_AT, OUT_ROWS = 4 * HD, 4 * HD + 32
PG_COLS = 10
PG_ROWS = 80
PG_USED = 208
NEAR = (0, 2, 7, 1)

NT = (((1,), (1,)), ((), ()))
TN = (((0,), (0,)), ((), ()))
NN = (((1,), (0,)), ((), ()))


def dot(left, right, dims):
    return lax.dot_general(left, right, dims, preferred_element_type=jnp.float32)


def pack_keys_kernel(k_hbm, v_hbm, out_hbm, k_ref, v_ref, out_ref, in_sems, out_sems):
    arrays = ((k_hbm, k_ref, K_AT), (v_hbm, v_ref, V_AT))
    loads = []
    for j in range(HEADS_HERE):
        cols = pl.ds(j * HD, HD)
        for i, (hbm, ref, _) in enumerate(arrays):
            load = pltpu.make_async_copy(hbm.at[cols], ref.at[cols], in_sems.at[j, i])
            load.start()
            loads.append(load)
    stores = []
    for j in range(HEADS_HERE):
        for i, (_, ref, first) in enumerate(arrays):
            loads[2 * j + i].wait()
            for b in range(2):
                at = first + b * HD
                block = ref[j * HD : (j + 1) * HD, b * HALF : (b + 1) * HALF]
                out_ref[j, at : at + HD] = block
        for h in range(2):
            there = h * HEADS_HERE + j
            store = pltpu.make_async_copy(out_ref.at[j], out_hbm.at[there], out_sems.at[there])
            store.start()
            stores.append(store)
    for store in stores:
        store.wait()


def pack_queries_kernel(q_hbm, o_hbm, cot_ref, w_ref, *refs):
    out_refs, (q_ref, o_ref, g_ref, extra_ref, sems) = refs[: len(NEAR)], refs[len(NEAR) :]
    pairs = ((q_hbm, q_ref), (o_hbm, o_ref))
    copies = [pltpu.make_async_copy(x, y, sems.at[i]) for i, (x, y) in enumerate(pairs)]
    for copy in copies:
        copy.start()
    g_ref[...] = dot(w_ref[...], cot_ref[...], NN).astype(jnp.bfloat16)
    for copy in copies:
        copy.wait()
    for j in range(HEADS_HERE):
        cols = slice(j * HD, (j + 1) * HD)
        delta = jnp.sum(
            g_ref[cols].astype(jnp.float32) * o_ref[cols].astype(jnp.float32),
            axis=0,
            keepdims=True,
        )
        high = delta.astype(jnp.bfloat16).astype(jnp.float32)
        rest = delta - high
        middle = rest.astype(jnp.bfloat16).astype(jnp.float32)
        low = rest - middle
        row = lax.broadcasted_iota(jnp.int32, (EXT - HD, ROWS), 0)
        extra = jnp.where(
            row == 0, high, jnp.where(row == 1, middle, jnp.where(row == 2, low, 0.0))
        )
        extra_ref[j * (EXT - HD) : (j + 1) * (EXT - HD)] = extra.astype(jnp.bfloat16)
    here = lax.axis_index("ctx")
    for away, ref in zip(NEAR, out_refs):
        j = lax.rem(here + away, HEADS_HERE)
        cols = pl.ds(pl.multiple_of(j * HD, 16), HD)
        ref[:HD] = q_ref[cols]
        ref[HD : 2 * HD] = g_ref[cols]
        rows = pl.ds(pl.multiple_of(j * (EXT - HD), 16), EXT - HD)
        ref[2 * HD :] = extra_ref[rows]


def proj_kernel(cot_ref, o_ref, kept_ref, given_ref, term_ref):
    upper = lax.rem(lax.axis_index("dp"), 2)
    empty = jnp.zeros((PG_USED - 200, HALF), jnp.float32)
    term_ref[...] = dot(cot_ref[...], o_ref[...], NT)
    for ref, wanted in ((given_ref, 1 - upper), (kept_ref, upper)):
        for k in range(SHARDS):
            start = pl.multiple_of((2 * k + wanted) * PG_ROWS, 8)
            part = term_ref[pl.ds(start, PG_ROWS)]
            for c in range(2):
                at = c * PG_ROWS
                ref[k, at : at + PG_ROWS] = part[:, HALF * c : HALF * (c + 1)].astype(ref.dtype)
            last = part[:, 2 * HALF :]
            last = jnp.concatenate([last[: PG_ROWS // 2], last[PG_ROWS // 2 :]], axis=1)
            ref[k, 2 * PG_ROWS :] = jnp.concatenate([last, empty], axis=0).astype(ref.dtype)


def add_kernel(kept_ref, taken_ref, out_ref):
    out_ref[...] = (kept_ref[...] + taken_ref[...].astype(jnp.float32)).astype(jnp.bfloat16)


def after_kernel(*refs):
    pass


def add_share_kernel(parts_ref, sent_in_ref, sent_ref, pieces, sem):
    total = parts_ref[0].astype(jnp.float32)
    for k in range(1, SHARDS):
        total = total + parts_ref[k].astype(jnp.float32)
    empty = jnp.zeros((1, HALF), jnp.float32)
    for s in range(SHARDS):
        blocks = [total[c * PG_ROWS + s * PG_COLS :][:PG_COLS] for c in range(2)]
        third = total[2 * PG_ROWS + s % 4 * PG_COLS :][:PG_COLS, s // 4 * 64 :][:, :64]
        blocks.append(jnp.concatenate([third[:5], third[5:]], axis=1))
        first = jnp.concatenate([blocks[0], blocks[2], empty], axis=0)
        second = jnp.concatenate([blocks[1], jnp.zeros((6, HALF), jnp.float32)], axis=0)
        pieces[s] = jnp.concatenate([first, second], axis=0).astype(jnp.bfloat16)
    copy = pltpu.make_async_copy(pieces, sent_ref.at[:, pl.ds(PG_AT, OUT_ROWS - PG_AT)], sem)
    copy.start()
    copy.wait()


def grad_kernel(x_ref, *refs):
    near, (out_ref, *dq_refs) = refs[: len(NEAR)], refs[len(NEAR) : 2 * len(NEAR) + 1]
    k_t, v_t, dk, dv = refs[2 * len(NEAR) + 1 :]
    for s in range(SHARDS):
        for b in range(2):
            tokens = slice((2 * s + b) * HALF, (2 * s + b + 1) * HALF)
            k_t[:, tokens] = x_ref[s, K_AT + b * HD : K_AT + (b + 1) * HD]
            v_t[:HD, tokens] = x_ref[s, V_AT + b * HD : V_AT + (b + 1) * HD]
    row = lax.broadcasted_iota(jnp.int32, (EXT - HD, SHARDS * ROWS), 0)
    v_t[HD:] = jnp.where(row < 3, -1.0, 0.0).astype(jnp.bfloat16)
    for i, (block, dq_ref) in enumerate(zip(near, dq_refs)):
        q, g = block[:HD], block[HD:]
        scores = dot(q, k_t[...], TN)
        peak = jnp.max(scores, axis=1, keepdims=True) * (FACTOR * LOG2E)
        raised = jnp.exp2(scores * (FACTOR * LOG2E) - peak)
        prob = raised * (1.0 / jnp.sum(raised, axis=1, keepdims=True))
        shifted = dot(g, v_t[...], TN)
        dscore = (prob * shifted).astype(jnp.bfloat16)
        dv_part = dot(g[:HD], prob.astype(jnp.bfloat16), NN)
        dk_part = dot(q, dscore, NN)
        if i == 0:
            dv[...] = dv_part
            dk[...] = dk_part
        else:
            dv[...] += dv_part
            dk[...] += dk_part
        dq_ref[...] = (dot(k_t[...], dscore, NT) * FACTOR).astype(jnp.bfloat16)
    for s in range(SHARDS):
        for b in range(2):
            tokens = slice((2 * s + b) * HALF, (2 * s + b + 1) * HALF)
            at = b * HD
            out_ref[s, K_AT + at : K_AT + at + HD] = (dk[:, tokens] * FACTOR).astype(jnp.bfloat16)
            out_ref[s, V_AT + at : V_AT + at + HD] = dv[:, tokens].astype(jnp.bfloat16)


def unpack_kernel(x_ref, *refs):
    near, (dq_ref, dk_ref, dv_ref, pg_ref) = refs[: len(NEAR)], refs[len(NEAR) :]
    here = lax.axis_index("ctx")
    for away, ref in zip(NEAR, near):
        j = lax.rem(here + away, HEADS_HERE)
        dq_ref[pl.ds(pl.multiple_of(j * HD, 16), HD)] = ref[...]
    for j in range(HEADS_HERE):
        for ref, start in ((dk_ref, K_AT), (dv_ref, V_AT)):
            for b in range(2):
                rows = slice(start + b * HD, start + (b + 1) * HD)
                total = x_ref[j, rows].astype(jnp.float32)
                total = total + x_ref[HEADS_HERE + j, rows].astype(jnp.float32)
                total = total.astype(jnp.bfloat16)
                ref[j * HD : (j + 1) * HD, b * HALF : (b + 1) * HALF] = total
    total = x_ref[0, PG_AT:].astype(jnp.float32)
    for s in range(1, SHARDS):
        total = total + x_ref[s, PG_AT:].astype(jnp.float32)
    last = total[PG_COLS : PG_COLS + 5]
    last = jnp.concatenate([last[:, :64], last[:, 64:]], axis=0)
    pg_ref[...] = jnp.concatenate([total[:PG_COLS], total[16 : 16 + PG_COLS], last], axis=1)


def call(kernel, outs, flops, transcendentals=0, scratch=(), mib=48, **more):
    return pl.pallas_call(
        kernel,
        out_shape=outs,
        scratch_shapes=scratch,
        compiler_params=pltpu.CompilerParams(vmem_limit_bytes=mib * 1024 * 1024),
        cost_estimate=pl.CostEstimate(
            flops=flops, bytes_accessed=2 * 1024 * 1024, transcendentals=transcendentals
        ),
        **more,
    )


def shifted_round(x, away, back=False):
    pairs = [
        (z, (z - away if away == 2 and z % 2 == 0 else z + away) % SHARDS) for z in range(SHARDS)
    ]
    return lax.ppermute(x, "ctx", [pair[::-1] for pair in pairs] if back else pairs)


def on_device(queries, keys, values, saved_out, cotangent, proj_weight):
    half, single = jnp.bfloat16, jnp.float32
    shape = jax.ShapeDtypeStruct
    vmem, anywhere = pl.BlockSpec(memory_space=pltpu.VMEM), pl.BlockSpec(memory_space=pl.ANY)
    whole = pltpu.VMEM((WIDE, ROWS), half)
    q, k, v, o, cot = (x.T for x in (queries, keys, values, saved_out, cotangent))

    pairs = call(
        pack_keys_kernel,
        shape((SHARDS, KV_ROWS, HALF), half),
        0,
        scratch=[whole] * 2
        + [
            pltpu.VMEM((HEADS_HERE, KV_ROWS, HALF), half),
            pltpu.SemaphoreType.DMA((HEADS_HERE, 2)),
            pltpu.SemaphoreType.DMA((SHARDS,)),
        ],
        in_specs=[anywhere] * 2,
        out_specs=anywhere,
        mib=60,
    )(k, v)
    pairs = lax.all_to_all(pairs, "ctx", 0, 0, tiled=True)

    full_cot = lax.all_gather(cot, "tp", axis=0, tiled=True)
    flops = 2 * ROWS * WIDE * 4 * WIDE
    block = (SHARDS, PG_USED, HALF)
    kept, given = call(
        proj_kernel,
        (shape(block, single), shape(block, half)),
        flops,
        scratch=[pltpu.VMEM((DP * PG_ROWS, WIDE), single)],
    )(full_cot, o)
    taken = lax.ppermute(given, "dp", [(i, i ^ 1) for i in range(DP)])
    near = call(
        pack_queries_kernel,
        [shape((QG_ROWS, ROWS), half)] * len(NEAR),
        flops,
        scratch=[whole] * 3
        + [pltpu.VMEM((HEADS_HERE * (EXT - HD), ROWS), half), pltpu.SemaphoreType.DMA((2,))],
        in_specs=[anywhere] * 2 + [vmem] * 2,
        mib=48,
    )(q, o, full_cot, proj_weight)
    near = [near[0]] + [shifted_round(x, away) for away, x in zip(NEAR[1:], near[1:])]
    parts = call(add_kernel, shape(block, half), 0)(kept, taken)
    parts = call(
        after_kernel,
        shape(block, half),
        0,
        in_specs=[anywhere] * len(near),
        out_specs=anywhere,
        input_output_aliases={0: 0},
    )(parts, *near[1:])
    along_y = [list(range(x, DP, 2)) for x in range(2)]
    parts = lax.all_to_all(parts, "dp", 0, 0, tiled=True, axis_index_groups=along_y)

    tokens = SHARDS * ROWS
    sent, *dq = call(
        grad_kernel,
        [shape((SHARDS, OUT_ROWS, HALF), half)]
        + [shape((HD, ROWS), half)] * len(NEAR),
        5 * 2 * tokens * (tokens // 2) * HD,
        tokens * (tokens // 2),
        [
            pltpu.VMEM((HD, tokens), half),
            pltpu.VMEM((EXT, tokens), half),
            pltpu.VMEM((HD, tokens), single),
            pltpu.VMEM((HD, tokens), single),
        ],
    )(pairs, *near)
    sent = call(
        add_share_kernel,
        shape(sent.shape, half),
        0,
        scratch=[
            pltpu.VMEM((SHARDS, OUT_ROWS - PG_AT, HALF), half),
            pltpu.SemaphoreType.DMA,
        ],
        in_specs=[vmem, anywhere],
        out_specs=anywhere,
        input_output_aliases={1: 0},
    )(parts, sent)
    back = lax.all_to_all(sent, "ctx", 0, 0, tiled=True)
    dq = [dq[0]] + [shifted_round(x, away, back=True) for away, x in zip(NEAR[1:], dq[1:])]
    grad = shape((WIDE, ROWS), half)
    outs = call(unpack_kernel, (grad, grad, grad, shape((PG_COLS, WIDE), single)), 0)(back, *dq)
    return tuple(x.T for x in outs)


def solution(mesh):
    rows = P(("dp", "ctx"), "tp")
    return jax.shard_map(
        on_device,
        mesh=mesh,
        in_specs=(rows, rows, rows, rows, rows, P("tp", None)),
        out_specs=(rows, rows, rows, P("tp", ("dp", "ctx"))),
        check_vma=False,
    )
```
